128 devices in a mesh: tm: 8 (over z, x_hi), height: 16 (over y, x_lo, core).
Axes of the slice: x: 4 (x_hi: 2, x_lo: 2; x = x_hi * 2 + x_lo), y: 4, z: 4, core: 2. Of those that a mesh axis runs over, the one named last changes fastest.
Arguments:
- queries: bfloat16 [16, 16, 160, 2560], P('tm', 'height'), may hold values from -6 to 6
- keys: bfloat16 [16, 16, 160, 2560], P('tm', 'height'), may hold values from -6 to 6
- values: bfloat16 [16, 16, 160, 2560], P('tm', 'height'), may hold values from -6 to 6
- head_window_radius: int32 [20, 3], replicated, may hold values from 0 to 2, as said below
- output_weight: bfloat16 [2560, 2560], P('height'), may hold values from -0.125 to 0.125
- adapter_down_weight: bfloat16 [2560, 64], replicated, may hold values from -0.125 to 0.125
- adapter_up_weight: bfloat16 [64, 2560], replicated, may hold values from -0.75 to 0.75
- output_gradient: bfloat16 [16, 16, 160, 2560], P('tm', 'height'), may hold values from -6 to 6
Outputs:
- mixed: bfloat16 [16, 16, 160, 2560], P('tm', 'height')
- attention_gradient: bfloat16 [16, 16, 160, 2560], P('tm', 'height')
- grad_up: float32 [64, 2560], replicated
- grad_down: float32 [2560, 64], replicated
The draws below stay inside these ranges and needn't reach their ends.
Inputs may be any that keep to these rules, and one draw needn't show every extreme that they name: `head_window_radius`: radii along frames and rows are 0 or 1, along columns 0 to 2; along each axis some head has the largest radius.
All inputs are finite; a program needn't handle non-finite values.
Results may differ from the reference program's by a relative error of at most 0.0063.
Values may be sent and summed in bfloat16 or wider, within the bound.
A program may use at most 128 MiB of HBM per device.

```python
import math
import jax
import jax.numpy as jnp
from jax import lax

HEADS = 20
HEAD_DIM = 128
OUTPUT_FEATURES = 2560
ADAPTER_RANK = 64
TILE_W = 16
RW_MAX = 2
COLS = 160
ATTENTION_WIDTH = 2560
NF = 16
NR = 16


def draw_head_window_radius(key, part):
    key = jax.random.fold_in(key, 7)
    first_key, second_key = jax.random.split(key)
    limits = jnp.array([1, 1, RW_MAX], dtype=jnp.int32)
    radius = jax.random.randint(first_key, (HEADS, 3), 0, limits[None, :] + 1)
    chosen = jax.random.randint(second_key, (3,), 0, HEADS)
    radius = radius.at[chosen, jnp.arange(3)].set(limits)
    return radius.astype(jnp.int32)


def draw_queries(key, part):
    key = jax.random.fold_in(key, 1)
    base = jnp.clip(jax.random.normal(key, (NF, NR, COLS, HEADS * HEAD_DIM), jnp.float32), -6.0, 6.0)
    return base.astype(jnp.bfloat16)


def draw_keys(key, part):
    key = jax.random.fold_in(key, 2)
    base = jnp.clip(jax.random.normal(key, (NF, NR, COLS, HEADS * HEAD_DIM), jnp.float32), -6.0, 6.0)
    return base.astype(jnp.bfloat16)


def level_of(rng, extent, cuts, low, high):
    level = 1.0
    for dim, parts in cuts:
        draws = jax.random.uniform(jax.random.fold_in(jax.random.fold_in(rng, 6), dim), (parts,), jnp.float32, low / len(cuts), high / len(cuts))
        level = level * jnp.repeat(jnp.exp(draws), extent[dim] // parts).reshape((-1,) + (1,) * (len(extent) - 1 - dim))
    return level


def centred(rng, extent, deviation, bound, cuts=(), kind=jnp.bfloat16):
    values = jax.random.normal(rng, extent, jnp.float32) * deviation
    if len(cuts) > 0:
        values = level_of(rng, extent, cuts, -0.22, 0.18) * values
    return jnp.clip(values, min=-bound, max=bound).astype(kind)


def setup_inputs(seed: int = 0) -> dict:
    key_of = jax.random.split(jax.random.key(seed), 9)
    queries = draw_queries(jax.random.fold_in(key_of[8], 71), 0)
    keys = draw_keys(jax.random.fold_in(key_of[8], 71), 0)
    values = centred(key_of[2], (NF, NR, COLS, ATTENTION_WIDTH), 1.0, 6.0, ((0, 8), (1, 16)))
    head_window_radius = draw_head_window_radius(jax.random.fold_in(key_of[8], 71), 0)
    output_weight = centred(key_of[4], (ATTENTION_WIDTH, OUTPUT_FEATURES), ATTENTION_WIDTH ** -0.5, 0.125, ((0, 16),))
    adapter_down_weight = centred(key_of[5], (ATTENTION_WIDTH, ADAPTER_RANK), ATTENTION_WIDTH ** -0.5, 0.125)
    adapter_up_weight = centred(key_of[6], (ADAPTER_RANK, OUTPUT_FEATURES), ADAPTER_RANK ** -0.5, 0.75)
    output_gradient = centred(key_of[7], (NF, NR, COLS, OUTPUT_FEATURES), 1.0, 6.0, ((0, 8), (1, 16)))
    return dict(queries=queries, keys=keys, values=values, head_window_radius=head_window_radius, output_weight=output_weight, adapter_down_weight=adapter_down_weight, adapter_up_weight=adapter_up_weight, output_gradient=output_gradient)


ADAPTER_SCALE = 2.0

def reference(queries, keys, values, head_window_radius, output_weight, adapter_down_weight, adapter_up_weight, output_gradient):
    frame_total, row_total, column_count, feature_width = queries.shape
    key_value = jnp.stack([keys, values])
    padded = jnp.pad(key_value, ((0, 0), (1, 1), (1, 1), (0, 0), (0, 0)))
    offsets = jnp.arange(3, dtype=jnp.int32) - 1
    col_tile = jnp.arange(column_count, dtype=jnp.int32) // TILE_W
    key_tile = jnp.tile(col_tile, 9)
    diff_tile = jnp.abs(col_tile[:, None] - key_tile[None, :])
    key_dframe = jnp.broadcast_to(jnp.abs(offsets)[:, None, None], (3, 3, column_count)).reshape(-1)
    key_drow = jnp.broadcast_to(jnp.abs(offsets)[None, :, None], (3, 3, column_count)).reshape(-1)
    radius_frame = head_window_radius[:, 0]
    radius_row = head_window_radius[:, 1]
    radius_col = head_window_radius[:, 2]
    zero_index = jnp.zeros((), jnp.int32)
    allowed_base = (key_dframe[None, None, :] <= radius_frame[:, None, None]) & (key_drow[None, None, :] <= radius_row[:, None, None]) & (diff_tile[None, :, :] <= radius_col[:, None, None])

    def block(index):
        frame = (index // row_total).astype(jnp.int32)
        row_at = (index % row_total).astype(jnp.int32)
        near = lax.dynamic_slice(padded, (zero_index, frame, row_at, zero_index, zero_index), (2, 3, 3, column_count, feature_width))
        frame_ids = frame + offsets
        row_ids = row_at + offsets
        frame_ok = (frame_ids >= 0) & (frame_ids < frame_total)
        row_ok = (row_ids >= 0) & (row_ids < row_total)
        valid = jnp.broadcast_to(frame_ok[:, None, None] & row_ok[None, :, None], (3, 3, column_count)).reshape(-1)
        query_block = lax.dynamic_slice(queries, (frame, row_at, zero_index, zero_index), (1, 1, column_count, feature_width))
        query_block = query_block.reshape(column_count, HEADS, HEAD_DIM).astype(jnp.float32)
        key_block = near[0].reshape(9 * column_count, HEADS, HEAD_DIM).astype(jnp.float32)
        value_block = near[1].reshape(9 * column_count, HEADS, HEAD_DIM).astype(jnp.float32)
        scores = jnp.einsum('qhd,khd->hqk', query_block, key_block) / math.sqrt(HEAD_DIM)
        allowed = allowed_base & valid[None, None, :]
        scores = jnp.where(allowed, scores, -1e+30)
        highest = lax.optimization_barrier(jnp.max(scores, axis=-1, keepdims=True))
        weights = jnp.exp(scores - highest)
        weights = weights / lax.optimization_barrier(jnp.sum(weights, axis=-1, keepdims=True))
        weights = weights.astype(jnp.bfloat16).astype(jnp.float32)
        result = jnp.einsum('hqk,khd->qhd', weights, value_block)
        return result.reshape(column_count, feature_width).astype(jnp.bfloat16)
    attention_output = lax.map(block, jnp.arange(frame_total * row_total, dtype=jnp.int32))
    attention_output = attention_output.reshape(frame_total * row_total * column_count, feature_width)
    output_cotangent = output_gradient.reshape(frame_total * row_total * column_count, OUTPUT_FEATURES)
    low_rank_product = jnp.dot(attention_output, adapter_down_weight, preferred_element_type=jnp.float32).astype(jnp.bfloat16)
    mixed = jnp.dot(attention_output, output_weight, preferred_element_type=jnp.float32) + ADAPTER_SCALE * jnp.dot(low_rank_product, adapter_up_weight, preferred_element_type=jnp.float32)
    low_rank_backward = jnp.dot(output_cotangent, adapter_up_weight.T, preferred_element_type=jnp.float32).astype(jnp.bfloat16)
    attention_gradient = jnp.dot(output_cotangent, output_weight.T, preferred_element_type=jnp.float32) + ADAPTER_SCALE * jnp.dot(low_rank_backward, adapter_down_weight.T, preferred_element_type=jnp.float32)
    adapter_factor = ADAPTER_SCALE / math.sqrt(frame_total * row_total * column_count)
    grad_up = adapter_factor * jnp.dot(low_rank_product.T, output_cotangent, preferred_element_type=jnp.float32)
    grad_down = adapter_factor * jnp.dot(attention_output.T, low_rank_backward, preferred_element_type=jnp.float32)
    mixed = mixed.astype(jnp.bfloat16).reshape(frame_total, row_total, column_count, OUTPUT_FEATURES)
    attention_gradient = attention_gradient.astype(jnp.bfloat16).reshape(frame_total, row_total, column_count, feature_width)
    return (mixed, attention_gradient, grad_up, grad_down)
```

```python
import functools
import math

import jax
import jax.numpy as jnp
from jax import lax
from jax.experimental import pallas as pl
from jax.experimental.pallas import tpu as pltpu
from jax.sharding import PartitionSpec as P

HEADS = 20
HEAD_DIM = 128
TILE_W = 16
COLS = 160
HALF = COLS // 2
WINDOW = 128
RANK = 64
ADAPTER_SCALE = 2.0
GRID = 16
CHIPS = 4
GROUP_HEADS = HEADS // CHIPS
GROUP = GROUP_HEADS * HEAD_DIM
WIDTH = HEADS * HEAD_DIM
NEG = -1e30
MESH = pl.DeviceIdType.MESH
BF = jnp.bfloat16
F32 = jnp.float32


def place():
    tm, height = lax.axis_index("tm"), lax.axis_index("height")
    z, xh = tm // 2, tm % 2
    y, xl, core = height // 4, (height // 2) % 2, height % 2
    return z, xh, y, xl, core


def device(z, x, y, core):
    return (z * 2 + x // 2, y * 4 + (x % 2) * 2 + core)


def enter(partners):
    barrier = pltpu.get_barrier_semaphore()
    for partner in partners:
        pl.semaphore_signal(barrier, inc=1, device_id=partner, device_id_type=MESH)
    pl.semaphore_wait(barrier, len(partners))


def remote(src, dst, send, recv, target):
    return pltpu.make_async_remote_copy(
        src_ref=src, dst_ref=dst, send_sem=send, recv_sem=recv, device_id=target, device_id_type=MESH
    )


def arrived(dst, sem):
    pltpu.make_async_copy(dst, dst, sem).wait()


def group_columns(x):
    return pl.ds(pl.multiple_of(x * GROUP, 128), GROUP)


def spread_kernel(q_ref, k_ref, v_ref, qs_ref, ks_ref, vs_ref, out_sem, in_sem, halo_out, halo_in):
    z, xh, y, xl, core = place()
    x = xh * 2 + xl
    here = xl == core
    band = y * 2 + core
    before, after = (band + 7) % 8, (band + 1) % 8
    up, down = device((z + 3) % 4, x, y, core), device((z + 1) % 4, x, y, core)
    left = device(z, x, before // 2, before % 2)
    right = device(z, x, after // 2, after % 2)
    ring = x * 2 + core
    partners = []
    for step in range(1, 8):
        other = (ring + step) % 8
        partners.append(device(z, other // 2, y, other % 2))
    outside = (band + 7 + 2 * core) % 8
    partners += [up, down, device(z, x, outside // 2, outside % 2)]
    enter(partners)

    arrays = ((k_ref, ks_ref, 1), (v_ref, vs_ref, 1), (q_ref, qs_ref, 0))

    def exchange(i, step):
        src, dst, pad = arrays[i]
        target = (x + step) % CHIPS
        piece = src.at[:, 0, :, group_columns(target)]
        slot = dst.at[pl.ds(pad + 2 * xh, 2), pad + core]
        return piece, slot, remote(
            piece, slot, out_sem.at[i, step], in_sem.at[i, xh * 2 + core], device(z, target, y, xl)
        )

    for i in range(3):
        for step in (2, 1, 3):
            exchange(i, step)[2].start()
        piece, slot, copy = exchange(i, 0)

        @pl.when(here)
        def _():
            pltpu.make_async_copy(piece, slot, in_sem.at[i, xh * 2 + core]).start()

        @pl.when(jnp.logical_not(here))
        def _():
            copy.start()

    def landed(i):
        _, dst, pad = arrays[i]
        for source in range(4):
            arrived(dst.at[pl.ds(pad + 2 * (source // 2), 2), pad + source % 2], in_sem.at[i, source])

    def halos(i):
        ref = arrays[i][1]

        def send(n, src, dst, target):
            return remote(src, dst, halo_out.at[i, n], halo_in.at[i, n], target)

        rows = pl.ds(1, 2)
        own = pl.ds(1, 4)
        first = [
            send(0, ref.at[1, rows], ref.at[5, rows], up),
            send(1, ref.at[4, rows], ref.at[0, rows], down),
            send(2, ref.at[own, 1], ref.at[own, 3], left),
            send(3, ref.at[own, 2], ref.at[own, 0], right),
        ]
        second = [
            send(4, ref.at[0, 1], ref.at[0, 3], left),
            send(5, ref.at[5, 1], ref.at[5, 3], left),
            send(6, ref.at[0, 2], ref.at[0, 0], right),
            send(7, ref.at[5, 2], ref.at[5, 0], right),
        ]
        return first, second

    halo = [halos(0), halos(1)]
    for i in range(2):
        landed(i)
        for copy in halo[i][0]:
            copy.start()
    for i in range(2):
        halo[i][0][0].wait_recv()
        halo[i][0][1].wait_recv()
        for copy in halo[i][1]:
            copy.start()
    landed(2)
    for i in range(2):
        first, second = halo[i]
        for copy in first[2:] + second:
            copy.wait_recv()
        for copy in first + second:
            copy.wait_send()
    for i in range(3):
        for step in (2, 1, 3):
            exchange(i, step)[2].wait_send()
        copy = exchange(i, 0)[2]

        @pl.when(jnp.logical_not(here))
        def _():
            copy.wait_send()


def spread(queries, keys, values):
    any_space = pl.BlockSpec(memory_space=pl.ANY)
    halo_shape = jax.ShapeDtypeStruct((6, 4, COLS, GROUP), BF)
    return pl.pallas_call(
        spread_kernel,
        out_shape=(jax.ShapeDtypeStruct((4, 2, COLS, GROUP), BF), halo_shape, halo_shape),
        in_specs=[any_space] * 3,
        out_specs=(any_space,) * 3,
        scratch_shapes=[
            pltpu.SemaphoreType.DMA((3, 4)),
            pltpu.SemaphoreType.DMA((3, 4)),
            pltpu.SemaphoreType.DMA((2, 8)),
            pltpu.SemaphoreType.DMA((2, 8)),
        ],
        compiler_params=pltpu.CompilerParams(collective_id=0, has_side_effects=True),
        cost_estimate=pl.CostEstimate(flops=0, bytes_accessed=200_000_000, transcendentals=0),
        name="spread_heads",
    )(queries, keys, values)


def attention_kernel(radius_ref, q_ref, k_ref, v_ref, o_ref):
    z, xh, y, xl, core = place()
    head = (xh * 2 + xl) * GROUP_HEADS + pl.program_id(0)
    f = pl.program_id(1)
    frame = z * 4 + f
    row_first = y * 4 + core * 2
    radius_frame = radius_ref[head * 3]
    radius_row = radius_ref[head * 3 + 1]
    radius_column = radius_ref[head * 3 + 2]
    scale = math.log2(math.e) / math.sqrt(HEAD_DIM)

    def attend(reach_frame, reach_row):
        for half in range(2):
            start = (COLS - WINDOW) * half
            query_tile = (lax.broadcasted_iota(jnp.int32, (HALF, WINDOW), 0) + half * HALF) // TILE_W
            key_tile = (lax.broadcasted_iota(jnp.int32, (HALF, WINDOW), 1) + start) // TILE_W
            near = jnp.abs(query_tile - key_tile) <= radius_column
            for r in range(2):
                q = q_ref[0, r, pl.ds(half * HALF, HALF), :]
                scores, values = [], []
                for df in range(-reach_frame, reach_frame + 1):
                    for dr in range(-reach_row, reach_row + 1):
                        k = k_ref[f + 1 + df, r + 1 + dr, pl.ds(start, WINDOW), :]
                        values.append(v_ref[f + 1 + df, r + 1 + dr, pl.ds(start, WINDOW), :])
                        s = lax.dot_general(
                            q, k, (((1,), (1,)), ((), ())), preferred_element_type=F32
                        )
                        allowed = near
                        if df != 0 or dr != 0:
                            row = row_first + r + dr
                            inside = (
                                (frame + df >= 0) & (frame + df < GRID) & (row >= 0) & (row < GRID)
                            )
                            allowed = near & inside
                        scores.append(jnp.where(allowed, s, NEG))
                highest = functools.reduce(jnp.maximum, scores)
                highest = jnp.max(highest, axis=1, keepdims=True)
                weights = [jnp.exp2((s - highest) * scale) for s in scores]
                total = jnp.sum(functools.reduce(jnp.add, weights), axis=1, keepdims=True)
                weights = jnp.concatenate([w.astype(BF) for w in weights], axis=1)
                result = jnp.dot(
                    weights, jnp.concatenate(values, axis=0), preferred_element_type=F32
                )
                o_ref[0, r, pl.ds(half * HALF, HALF), :] = (result / total).astype(BF)

    for reach_frame in range(2):
        for reach_row in range(2):

            @pl.when((radius_frame == reach_frame) & (radius_row == reach_row))
            def _():
                attend(reach_frame, reach_row)


def attention(radius, qs, ks, vs):
    wide = pl.BlockSpec((6, 4, COLS, HEAD_DIM), lambda h, f, radius: (0, 0, 0, h))
    narrow = pl.BlockSpec((1, 2, COLS, HEAD_DIM), lambda h, f, radius: (f, 0, 0, h))
    return pl.pallas_call(
        attention_kernel,
        out_shape=jax.ShapeDtypeStruct((4, 2, COLS, GROUP), BF),
        grid_spec=pltpu.PrefetchScalarGridSpec(
            num_scalar_prefetch=1,
            grid=(GROUP_HEADS, 4),
            in_specs=[narrow, wide, wide],
            out_specs=narrow,
        ),
        compiler_params=pltpu.CompilerParams(vmem_limit_bytes=40 * 2**20),
        cost_estimate=pl.CostEstimate(
            flops=3_000_000_000, bytes_accessed=14_000_000, transcendentals=3_000_000
        ),
        name="attend",
    )(radius.reshape(-1), qs, ks, vs)


def finish_kernel(
    factor, o_ref, w_hbm, g_ref, down_ref, up_ref, mixed_ref, back_ref, grads_ref,
    w_ref, att_ref, part_ref, ra_ref, acc_ref, rb_ref, sum_ref, rc_ref, rd_ref, fin_ref,
    w_sem, o_out, o_in, a_out, a_in, b_out, b_in, c_out, c_in, d_out, d_in, e_out, e_in,
):
    z, xh, y, xl, core = place()
    x = xh * 2 + xl
    here = xl == core
    ring = x * 2 + core
    load = pltpu.make_async_copy(w_hbm, w_ref, w_sem)
    load.start()

    def ring_device(step):
        other = (ring + step) % 8
        return other // 2, other % 2, device(z, other // 2, y, other % 2)

    def y_device(step):
        return device(z, x, (y + step) % 4, core)

    def z_device(step):
        return device((z + step) % 4, x, y, core)

    enter(
        [ring_device(step)[2] for step in range(1, 8)]
        + [y_device(step) for step in range(1, 4)]
        + [z_device(step) for step in range(1, 4)]
    )

    def give_back(n):
        frames = (xh + n // 2) % 2
        row = (core + n % 2) % 2
        piece = o_ref.at[pl.ds(2 * frames, 2), row]
        slot = att_ref.at[:, :, group_columns(x)]
        return piece, slot, remote(
            piece, slot, o_out.at[n], o_in.at[x], device(z, frames * 2 + core, y, row)
        )

    for n in (2, 3, 1):
        give_back(n)[2].start()
    piece, slot, copy = give_back(0)

    @pl.when(here)
    def _():
        pltpu.make_async_copy(piece, slot, o_in.at[x]).start()

    @pl.when(jnp.logical_not(here))
    def _():
        copy.start()

    contract_last = (((1,), (1,)), ((), ()))
    contract_first = (((0,), (0,)), ((), ()))
    tokens = 2 * COLS
    gradient = g_ref[...].reshape(tokens, WIDTH)
    low_back = lax.dot_general(
        gradient, up_ref[...], contract_last, preferred_element_type=F32
    ).astype(BF)
    load.wait()
    step_width = 256

    def backward(j, carry):
        rows = pl.ds(pl.multiple_of(j * step_width, step_width), step_width)
        frozen = lax.dot_general(
            g_ref[...].reshape(tokens, WIDTH), w_ref[rows, :], contract_last, preferred_element_type=F32
        )
        adapter = lax.dot_general(
            low_back, down_ref[rows, :], contract_last, preferred_element_type=F32
        )
        back_ref[:, :, rows] = (
            (frozen + ADAPTER_SCALE * adapter).astype(BF).reshape(2, COLS, step_width)
        )
        return carry

    lax.fori_loop(0, WIDTH // step_width, backward, 0)

    for source in range(CHIPS):
        arrived(att_ref.at[:, :, pl.ds(source * GROUP, GROUP)], o_in.at[source])
    attended = att_ref[...].reshape(tokens, WIDTH)
    low = jnp.dot(attended, down_ref[...], preferred_element_type=F32).astype(BF)
    part_ref[0] = (
        factor * lax.dot_general(low, gradient, contract_first, preferred_element_type=F32)
    ).astype(BF)
    part_ref[1] = (
        factor * lax.dot_general(low_back, attended, contract_first, preferred_element_type=F32)
    ).astype(BF)

    def phase_a(step):
        tx, tc, target = ring_device(step)
        return remote(
            part_ref.at[tc, :, group_columns(tx)], ra_ref.at[step - 1],
            a_out.at[step - 1], a_in.at[step - 1], target,
        )

    for step in range(1, 8):
        phase_a(step).start()

    def forward(j, carry):
        columns = pl.ds(pl.multiple_of(j * step_width, step_width), step_width)
        frozen = jnp.dot(
            att_ref[...].reshape(tokens, WIDTH), w_ref[:, columns], preferred_element_type=F32
        )
        adapter = jnp.dot(low, up_ref[:, columns], preferred_element_type=F32)
        mixed_ref[:, :, columns] = (
            (frozen + ADAPTER_SCALE * adapter).astype(BF).reshape(2, COLS, step_width)
        )
        return carry

    lax.fori_loop(0, WIDTH // step_width, forward, 0)

    total = part_ref[core, :, group_columns(x)].astype(F32)
    for step in range(1, 8):
        phase_a(step).wait_recv()
        total = total + ra_ref[step - 1].astype(F32)
    acc_ref[...] = total

    def chunk(n):
        return pl.ds(pl.multiple_of(n * 16, 16), 16)

    def phase_b(step):
        return remote(
            acc_ref.at[chunk((y + step) % 4)], rb_ref.at[step - 1],
            b_out.at[step - 1], b_in.at[step - 1], y_device(step),
        )

    for step in range(1, 4):
        phase_b(step).start()
    total = acc_ref[chunk(y), :]
    for step in range(1, 4):
        phase_b(step).wait_recv()
        total = total + rb_ref[step - 1]
    sum_ref[...] = total

    def phase_c(step):
        return remote(
            sum_ref, rc_ref.at[step - 1], c_out.at[step - 1], c_in.at[step - 1], z_device(step)
        )

    for step in range(1, 4):
        phase_c(step).start()
    for step in range(1, 4):
        phase_c(step).wait_recv()

    total = jnp.zeros((16, GROUP), F32)
    for source in range(4):
        back = (z - source + 4) % 4
        term = sum_ref[...]
        for step in range(1, 4):
            term = jnp.where(back == step, rc_ref[step - 1], term)
        total = total + term
    rd_ref[chunk(y), :] = total.astype(BF)

    def phase_d(step):
        return remote(
            rd_ref.at[chunk(y)], rd_ref.at[chunk(y)],
            d_out.at[step - 1], d_in.at[step - 1], y_device(step),
        )

    for step in range(1, 4):
        phase_d(step).start()
    for step in range(1, 4):
        arrived(rd_ref.at[chunk((y - step + 4) % 4)], d_in.at[step - 1])

    def phase_e(step):
        return remote(
            rd_ref, fin_ref.at[core, :, group_columns(x)],
            e_out.at[step - 1], e_in.at[step - 1], ring_device(step)[2],
        )

    for step in range(1, 8):
        phase_e(step).start()
    fin_ref[core, :, group_columns(x)] = rd_ref[...]
    for step in range(1, 8):
        other = (ring - step + 8) % 8
        arrived(fin_ref.at[other % 2, :, group_columns(other // 2)], e_in.at[step - 1])
    grads_ref[...] = fin_ref[...].astype(F32)

    for n in (2, 3, 1):
        give_back(n)[2].wait_send()
    copy = give_back(0)[2]

    @pl.when(jnp.logical_not(here))
    def _():
        copy.wait_send()

    for step in range(1, 8):
        phase_a(step).wait_send()
        phase_e(step).wait_send()
    for step in range(1, 4):
        phase_b(step).wait_send()
        phase_c(step).wait_send()
        phase_d(step).wait_send()


def finish(factor, attended, weight, gradient, down, up):
    whole = pl.BlockSpec(memory_space=pltpu.VMEM)
    any_space = pl.BlockSpec(memory_space=pl.ANY)
    block = jax.ShapeDtypeStruct((2, COLS, WIDTH), BF)
    dma = pltpu.SemaphoreType.DMA
    return pl.pallas_call(
        functools.partial(finish_kernel, factor),
        out_shape=(block, block, jax.ShapeDtypeStruct((2, RANK, WIDTH), F32)),
        in_specs=[any_space, any_space, whole, whole, whole],
        out_specs=(whole,) * 3,
        scratch_shapes=[
            pltpu.VMEM((WIDTH, WIDTH), BF),
            pltpu.VMEM((2, COLS, WIDTH), BF),
            pltpu.VMEM((2, RANK, WIDTH), BF),
            pltpu.VMEM((7, RANK, GROUP), BF),
            pltpu.VMEM((RANK, GROUP), F32),
            pltpu.VMEM((3, 16, GROUP), F32),
            pltpu.VMEM((16, GROUP), F32),
            pltpu.VMEM((3, 16, GROUP), F32),
            pltpu.VMEM((RANK, GROUP), BF),
            pltpu.VMEM((2, RANK, WIDTH), BF),
            dma, dma((4,)), dma((4,)), dma((7,)), dma((7,)), dma((3,)), dma((3,)),
            dma((3,)), dma((3,)), dma((3,)), dma((3,)), dma((7,)), dma((7,)),
        ],
        compiler_params=pltpu.CompilerParams(
            collective_id=1, has_side_effects=True, vmem_limit_bytes=48 * 2**20
        ),
        cost_estimate=pl.CostEstimate(
            flops=9_000_000_000, bytes_accessed=100_000_000, transcendentals=0
        ),
        name="project_and_reduce",
    )(attended, weight, gradient, down, up)


def per_device(
    queries, keys, values, head_window_radius, output_weight, adapter_down_weight, adapter_up_weight,
    output_gradient,
):
    weight = lax.all_gather(output_weight, "height", axis=0, tiled=True)
    qs, ks, vs = spread(queries, keys, values)
    attended = attention(head_window_radius, qs, ks, vs)
    factor = ADAPTER_SCALE / math.sqrt(GRID * GRID * COLS)
    mixed, back, grads = finish(
        factor, attended, weight, output_gradient.reshape(2, COLS, WIDTH), adapter_down_weight,
        adapter_up_weight,
    )
    shape = (2, 1, COLS, WIDTH)
    return mixed.reshape(shape), back.reshape(shape), grads[0], grads[1].T


def solution(mesh):
    tokens = P("tm", "height", None, None)
    return jax.shard_map(
        per_device,
        mesh=mesh,
        in_specs=(tokens, tokens, tokens, P(), P("height", None), P(), P(), tokens),
        out_specs=(tokens, tokens, P(), P()),
        check_vma=False,
    )
```

```python
import functools
import math

import jax
import jax.numpy as jnp
from jax import lax
from jax.experimental import pallas as pl
from jax.experimental.pallas import tpu as pltpu
from jax.sharding import PartitionSpec as P

HEADS = 20
HEAD_DIM = 128
TILE_W = 16
COLS = 160
HALF = COLS // 2
WINDOW = 128
RANK = 64
ADAPTER_SCALE = 2.0
GRID = 16
CHIPS = 4
GROUP_HEADS = HEADS // CHIPS
GROUP = GROUP_HEADS * HEAD_DIM
WIDTH = HEADS * HEAD_DIM
NEG = -1e30
MESH = pl.DeviceIdType.MESH
BF = jnp.bfloat16
F32 = jnp.float32


def place():
    tm, height = lax.axis_index("tm"), lax.axis_index("height")
    z, xh = tm // 2, tm % 2
    y, xl, core = height // 4, (height // 2) % 2, height % 2
    return z, xh, y, xl, core


def device(z, x, y, core):
    return (z * 2 + x // 2, y * 4 + (x % 2) * 2 + core)


def enter(partners):
    barrier = pltpu.get_barrier_semaphore()
    for partner in partners:
        pl.semaphore_signal(barrier, inc=1, device_id=partner, device_id_type=MESH)
    pl.semaphore_wait(barrier, len(partners))


def remote(src, dst, send, recv, target):
    return pltpu.make_async_remote_copy(
        src_ref=src, dst_ref=dst, send_sem=send, recv_sem=recv, device_id=target, device_id_type=MESH
    )


def arrived(dst, sem):
    pltpu.make_async_copy(dst, dst, sem).wait()


def group_columns(x):
    return pl.ds(pl.multiple_of(x * GROUP, 128), GROUP)


def attend(j, f, half, radii, frame, row_first, q_ref, k_ref, v_ref, o_ref):
    radius_frame, radius_row, radius_column = radii
    start = (COLS - WINDOW) * half
    query_tile = (lax.broadcasted_iota(jnp.int32, (HALF, WINDOW), 0) + half * HALF) // TILE_W
    key_tile = (lax.broadcasted_iota(jnp.int32, (HALF, WINDOW), 1) + start) // TILE_W
    near = jnp.abs(query_tile - key_tile) <= radius_column
    query_rows, key_rows = pl.ds(half * HALF, HALF), pl.ds(start, WINDOW)
    places = [(a, b) for a in range(3) for b in range(4)]
    q = jnp.concatenate([q_ref[j, f, r, query_rows, :] for r in range(2)], axis=0)
    k = jnp.concatenate([k_ref[j, f + a, b, key_rows, :] for a, b in places], axis=0)
    v = jnp.concatenate([v_ref[j, f + a, b, key_rows, :] for a, b in places], axis=0)
    scores = lax.dot_general(q, k, (((1,), (1,)), ((), ())), preferred_element_type=F32)
    scale = math.log2(math.e) / math.sqrt(HEAD_DIM)
    nothing = jnp.zeros((HALF, WINDOW), BF)
    rows = []
    for r in range(2):
        masked = {}
        for at, (a, b) in enumerate(places):
            if not r <= b <= r + 2:
                continue
            s = scores[r * HALF : (r + 1) * HALF, at * WINDOW : (at + 1) * WINDOW]
            allowed = near
            if a != 1 or b != r + 1:
                other_frame, other_row = frame + (a - 1), row_first + (b - 1)
                inside = (
                    (other_frame >= 0) & (other_frame < GRID) & (other_row >= 0) & (other_row < GRID)
                )
                if a != 1:
                    inside = inside & (radius_frame > 0)
                if b != r + 1:
                    inside = inside & (radius_row > 0)
                allowed = near & inside
            masked[a, b] = jnp.where(allowed, s, NEG)
        highest = jnp.max(functools.reduce(jnp.maximum, masked.values()), axis=1, keepdims=True)
        weights = {at: jnp.exp2((s - highest) * scale) for at, s in masked.items()}
        total = jnp.sum(functools.reduce(jnp.add, weights.values()), axis=1, keepdims=True)
        share = 1.0 / total
        rows.append(
            jnp.concatenate(
                [(weights[at] * share).astype(BF) if at in weights else nothing for at in places], axis=1
            )
        )
    result = jnp.dot(jnp.concatenate(rows, axis=0), v, preferred_element_type=F32).astype(BF)
    for r in range(2):
        o_ref[j, f, r, query_rows, :] = result[r * HALF : (r + 1) * HALF]


def step_kernel(
    factor, radius_ref, q_hbm, k_hbm, v_hbm, w_hbm, g_hbm, down_ref, up_ref,
    mixed_ref, back_ref, grads_ref,
    qs_ref, ks_ref, vs_ref, os_ref, w_ref, g_ref, att_ref,
    part_ref, ra_ref, acc_ref, rb_ref, sum_ref, rc_ref, rd_ref, fin_ref,
    load_sem, out_sem, in_sem, halo_out, halo_in, o_out, o_in,
    wx_sem, wy_out, wy_in, wz_out, wz_in, wf_out, wf_in, ws_out, ws_in,
    a_out, a_in, b_out, b_in, c_out, c_in, d_out, d_in, e_out, e_in,
):
    z, xh, y, xl, core = place()
    x = xh * 2 + xl
    here = xl == core
    ring = x * 2 + core
    band = y * 2 + core
    before, after = (band + 7) % 8, (band + 1) % 8
    left = device(z, x, before // 2, before % 2)
    right = device(z, x, after // 2, after % 2)
    sibling = device(z, x, y, 1 - core)

    def ring_device(step):
        other = (ring + step) % 8
        return other // 2, other % 2, device(z, other // 2, y, other % 2)

    def y_device(step):
        return device(z, x, (y + step) % 4, core)

    def z_device(step):
        return device((z + step) % 4, x, y, core)

    up, down = z_device(3), z_device(1)

    def head_columns(chip, j):
        return pl.ds(pl.multiple_of((chip * GROUP_HEADS + j) * HEAD_DIM, HEAD_DIM), HEAD_DIM)

    own_weight = w_ref.at[y * 2 + xl, core, :, group_columns(z)]
    load_gradient = pltpu.make_async_copy(g_hbm, g_ref, load_sem.at[0])
    load_weight = pltpu.make_async_copy(w_hbm.at[:, group_columns(z)], own_weight, load_sem.at[1])
    load_gradient.start()
    load_weight.start()

    outside = (band + 7 + 2 * core) % 8
    enter(
        [ring_device(step)[2] for step in range(1, 8)]
        + [y_device(step) for step in range(1, 4)]
        + [z_device(step) for step in range(1, 4)]
        + [device(z, x, outside // 2, outside % 2)]
    )

    arrays = ((k_hbm, ks_ref, 1), (v_hbm, vs_ref, 1), (q_hbm, qs_ref, 0))

    def exchange(i, j, step):
        src, dst, pad = arrays[i]
        target = (x + step) % CHIPS
        piece = src.at[:, 0, :, head_columns(target, j)]
        slot = dst.at[j, pl.ds(pad + 2 * xh, 2), pad + core]
        return piece, slot, remote(
            piece, slot, out_sem.at[i, j, step], in_sem.at[i, j, xh * 2 + core],
            device(z, target, y, xl),
        )

    def give(i, j):
        for step in (2, 1, 3):
            exchange(i, j, step)[2].start()
        piece, slot, copy = exchange(i, j, 0)

        @pl.when(here)
        def _():
            pltpu.make_async_copy(piece, slot, in_sem.at[i, j, xh * 2 + core]).start()

        @pl.when(jnp.logical_not(here))
        def _():
            copy.start()

    def landed(i, j):
        _, dst, pad = arrays[i]
        for source in range(4):
            arrived(
                dst.at[j, pl.ds(pad + 2 * (source // 2), 2), pad + source % 2], in_sem.at[i, j, source]
            )

    def halos(i, j):
        ref = arrays[i][1].at[j]

        def send(n, src, dst, target):
            return remote(src, dst, halo_out.at[i, j, n], halo_in.at[i, j, n], target)

        rows, own = pl.ds(1, 2), pl.ds(1, 4)
        return (
            send(0, ref.at[1, rows], ref.at[5, rows], up),
            send(1, ref.at[4, rows], ref.at[0, rows], down),
            send(2, ref.at[own, 1], ref.at[own, 3], left),
            send(3, ref.at[own, 2], ref.at[own, 0], right),
            send(4, ref.at[0, 1], ref.at[0, 3], left),
            send(5, ref.at[5, 1], ref.at[5, 3], left),
            send(6, ref.at[0, 2], ref.at[0, 0], right),
            send(7, ref.at[5, 2], ref.at[5, 0], right),
        )

    def start_halos(j):
        for i in range(2):
            landed(i, j)
            for copy in halos(i, j)[:4]:
                copy.start()

    def start_corners(j):
        for i in range(2):
            copies = halos(i, j)
            copies[0].wait_recv()
            copies[1].wait_recv()
            for copy in copies[4:]:
                copy.start()

    def await_head(j):
        for i in range(2):
            for copy in halos(i, j)[2:]:
                copy.wait_recv()
        landed(2, j)

    def attend_frames(j, first, last):
        head = x * GROUP_HEADS + j
        radii = [radius_ref[head, n] for n in range(3)]

        def one(f, carry):
            for half in range(2):
                attend(
                    j, f, half, radii, z * 4 + f, y * 4 + core * 2, qs_ref, ks_ref, vs_ref, os_ref
                )
            return carry

        lax.fori_loop(first, last, one, 0)

    def give_back(j, n):
        frames = (xh + n // 2) % 2
        row = (core + n % 2) % 2
        piece = os_ref.at[j, pl.ds(2 * frames, 2), row]
        slot = att_ref.at[:, :, head_columns(x, j)]
        return piece, slot, remote(
            piece, slot, o_out.at[j, n], o_in.at[j, x], device(z, frames * 2 + core, y, row)
        )

    def start_back(j):
        for n in (2, 3, 1):
            give_back(j, n)[2].start()
        piece, slot, copy = give_back(j, 0)

        @pl.when(here)
        def _():
            pltpu.make_async_copy(piece, slot, o_in.at[j, x]).start()

        @pl.when(jnp.logical_not(here))
        def _():
            copy.start()

    def weight_piece(quarter, n, side):
        return w_ref.at[pl.ds(2 * ((y + n) % 4), 2), side, :, group_columns((z + quarter) % 4)]

    weight_x = remote(
        own_weight, own_weight, wx_sem.at[0], wx_sem.at[1], device(z, xh * 2 + 1 - xl, y, core)
    )

    def weight_y(step):
        piece = weight_piece(0, 0, core)
        return remote(piece, piece, wy_out.at[step - 1], wy_in.at[3 - step], y_device(step))

    def weight_z(way, n):
        piece = weight_piece(0, n, core)
        return remote(piece, piece, wz_out.at[way, n], wz_in.at[way, n], (up, down)[way])

    def weight_forward(n):
        piece = weight_piece(3 if n < 2 else 1, n, core)
        return remote(piece, piece, wf_out.at[n], wf_in.at[n], down if n < 2 else up)

    def weight_sibling(quarter, n):
        piece = weight_piece(quarter, n, core)
        return remote(piece, piece, ws_out.at[quarter, n], ws_in.at[quarter, n], sibling)

    def spread_weight(n):
        weight_z(0, n).start()
        weight_z(1, n).start()
        weight_sibling(0, n).start()

    def take_weight_y(n):
        arrived(weight_piece(0, n, core), wy_in.at[n - 1])

    def pass_weight(n):
        arrived(weight_piece(1, n, core), wz_in.at[0, n])
        arrived(weight_piece(3, n, core), wz_in.at[1, n])
        weight_forward(n).start()
        weight_sibling(1, n).start()
        weight_sibling(3, n).start()

    def last_weight(n):
        arrived(weight_piece(2, n, core), wf_in.at[n])
        weight_sibling(2, n).start()

    K, V, Q = 0, 1, 2
    for i, j in ((K, 0), (V, 0), (K, 1), (V, 1), (Q, 0)):
        give(i, j)
    load_weight.wait()
    weight_x.start()
    load_gradient.wait()
    contract_last = (((1,), (1,)), ((), ()))
    contract_first = (((0,), (0,)), ((), ()))
    tokens = 2 * COLS
    low_back = lax.dot_general(
        g_ref[...].reshape(tokens, WIDTH), up_ref[...], contract_last, preferred_element_type=F32
    ).astype(BF)

    start_halos(0)
    for i, j in ((K, 2), (V, 2), (Q, 1)):
        give(i, j)
    weight_x.wait_recv()
    for step in (2, 1, 3):
        weight_y(step).start()
    spread_weight(0)
    start_corners(0)

    start_halos(1)
    for i, j in ((K, 3), (V, 3), (Q, 2)):
        give(i, j)
    await_head(0)
    attend_frames(0, 0, 4)
    start_back(0)
    start_corners(1)
    take_weight_y(1)
    spread_weight(1)
    take_weight_y(3)
    spread_weight(3)

    start_halos(2)
    for i, j in ((K, 4), (V, 4), (Q, 3), (Q, 4)):
        give(i, j)
    await_head(1)
    attend_frames(1, 0, 4)
    start_back(1)
    start_corners(2)
    take_weight_y(2)
    spread_weight(2)
    pass_weight(0)

    start_halos(3)
    await_head(2)
    attend_frames(2, 0, 4)
    start_back(2)
    start_corners(3)
    pass_weight(1)

    start_halos(4)
    await_head(3)
    attend_frames(3, 0, 2)
    start_corners(4)
    attend_frames(3, 2, 4)
    start_back(3)
    await_head(4)
    attend_frames(4, 0, 4)
    start_back(4)
    pass_weight(3)
    pass_weight(2)

    for j in range(GROUP_HEADS):
        for source in range(CHIPS):
            arrived(att_ref.at[:, :, head_columns(source, j)], o_in.at[j, source])
    low = jnp.dot(
        att_ref[...].reshape(tokens, WIDTH), down_ref[...], preferred_element_type=F32
    ).astype(BF)
    part_ref[0] = (
        factor
        * lax.dot_general(
            low, g_ref[...].reshape(tokens, WIDTH), contract_first, preferred_element_type=F32
        )
    ).astype(BF)
    part_ref[1] = (
        factor
        * lax.dot_general(
            low_back, att_ref[...].reshape(tokens, WIDTH), contract_first, preferred_element_type=F32
        )
    ).astype(BF)

    def phase_a(step):
        tx, tc, target = ring_device(step)
        return remote(
            part_ref.at[tc, :, group_columns(tx)], ra_ref.at[step - 1],
            a_out.at[step - 1], a_in.at[step - 1], target,
        )

    for step in range(1, 8):
        phase_a(step).start()

    step_width = 256

    def forward(j, carry):
        columns = pl.ds(pl.multiple_of(j * step_width, step_width), step_width)
        frozen = jnp.dot(
            att_ref[...].reshape(tokens, WIDTH), w_ref[:, :, :, columns].reshape(WIDTH, step_width),
            preferred_element_type=F32,
        )
        adapter = jnp.dot(low, up_ref[:, columns], preferred_element_type=F32)
        mixed_ref[:, :, columns] = (
            (frozen + ADAPTER_SCALE * adapter).astype(BF).reshape(2, COLS, step_width)
        )
        return carry

    def backward(j, carry):
        rows = group_columns(j)
        frozen = lax.dot_general(
            g_ref[...].reshape(tokens, WIDTH), w_ref[pl.ds(2 * j, 2)].reshape(GROUP, WIDTH),
            contract_last, preferred_element_type=F32,
        )
        adapter = lax.dot_general(
            low_back, down_ref[rows, :], contract_last, preferred_element_type=F32
        )
        back_ref[:, :, rows] = (
            (frozen + ADAPTER_SCALE * adapter).astype(BF).reshape(2, COLS, GROUP)
        )
        return carry

    def from_sibling(quarter):
        for n in range(4):
            arrived(weight_piece(quarter, n, 1 - core), ws_in.at[quarter, n])

    half_blocks = WIDTH // step_width // 2
    near_half = z // 2
    near_quarter = 1 + 2 * (z % 2)
    from_sibling(0)
    from_sibling(near_quarter)
    lax.fori_loop(near_half * half_blocks, (near_half + 1) * half_blocks, forward, 0)
    for n in (0, 1, 3, 2):
        last_weight(n)

    total = part_ref[core, :, group_columns(x)].astype(F32)
    for step in range(1, 8):
        phase_a(step).wait_recv()
        total = total + ra_ref[step - 1].astype(F32)
    acc_ref[...] = total

    def chunk(n):
        return pl.ds(pl.multiple_of(n * 16, 16), 16)

    def phase_b(step):
        return remote(
            acc_ref.at[chunk((y + step) % 4)], rb_ref.at[step - 1],
            b_out.at[step - 1], b_in.at[step - 1], y_device(step),
        )

    for step in range(1, 4):
        phase_b(step).start()
    total = acc_ref[chunk(y), :]
    for step in range(1, 4):
        phase_b(step).wait_recv()
        total = total + rb_ref[step - 1]
    sum_ref[...] = total

    def phase_c(step):
        return remote(
            sum_ref, rc_ref.at[step - 1], c_out.at[step - 1], c_in.at[step - 1], z_device(step)
        )

    for step in range(1, 4):
        phase_c(step).start()
    for step in range(1, 4):
        phase_c(step).wait_recv()

    total = jnp.zeros((16, GROUP), F32)
    for source in range(4):
        back = (z - source + 4) % 4
        term = sum_ref[...]
        for step in range(1, 4):
            term = jnp.where(back == step, rc_ref[step - 1], term)
        total = total + term
    rd_ref[chunk(y), :] = total.astype(BF)

    def phase_d(step):
        return remote(
            rd_ref.at[chunk(y)], rd_ref.at[chunk(y)],
            d_out.at[step - 1], d_in.at[step - 1], y_device(step),
        )

    for step in range(1, 4):
        phase_d(step).start()
    for step in range(1, 4):
        arrived(rd_ref.at[chunk((y - step + 4) % 4)], d_in.at[step - 1])

    def phase_e(step):
        return remote(
            rd_ref, fin_ref.at[core, :, group_columns(x)],
            e_out.at[step - 1], e_in.at[step - 1], ring_device(step)[2],
        )

    for step in range(1, 8):
        phase_e(step).start()
    fin_ref[core, :, group_columns(x)] = rd_ref[...]

    from_sibling(4 - near_quarter)
    from_sibling(2)
    lax.fori_loop((1 - near_half) * half_blocks, (2 - near_half) * half_blocks, forward, 0)
    lax.fori_loop(0, CHIPS, backward, 0)

    for step in range(1, 8):
        other = (ring - step + 8) % 8
        arrived(fin_ref.at[other % 2, :, group_columns(other // 2)], e_in.at[step - 1])
    grads_ref[...] = fin_ref[...].astype(F32)

    for j in range(GROUP_HEADS):
        for i in range(3):
            for step in (2, 1, 3):
                exchange(i, j, step)[2].wait_send()
        for i in range(2):
            for copy in halos(i, j):
                copy.wait_send()
        for n in (2, 3, 1):
            give_back(j, n)[2].wait_send()

    @pl.when(jnp.logical_not(here))
    def _():
        for j in range(GROUP_HEADS):
            for i in range(3):
                exchange(i, j, 0)[2].wait_send()
            give_back(j, 0)[2].wait_send()

    weight_x.wait_send()
    for step in range(1, 4):
        weight_y(step).wait_send()
    for n in range(4):
        weight_z(0, n).wait_send()
        weight_z(1, n).wait_send()
        weight_forward(n).wait_send()
        for quarter in range(4):
            weight_sibling(quarter, n).wait_send()
    for step in range(1, 8):
        phase_a(step).wait_send()
        phase_e(step).wait_send()
    for step in range(1, 4):
        phase_b(step).wait_send()
        phase_c(step).wait_send()
        phase_d(step).wait_send()


def per_device(
    queries, keys, values, head_window_radius, output_weight, adapter_down_weight, adapter_up_weight,
    output_gradient,
):
    factor = ADAPTER_SCALE / math.sqrt(GRID * GRID * COLS)
    vmem = pl.BlockSpec(memory_space=pltpu.VMEM)
    smem = pl.BlockSpec(memory_space=pltpu.SMEM)
    hbm = pl.BlockSpec(memory_space=pl.ANY)
    block = jax.ShapeDtypeStruct((2, COLS, WIDTH), BF)
    dma = pltpu.SemaphoreType.DMA
    mixed, back, grads = pl.pallas_call(
        functools.partial(step_kernel, factor),
        out_shape=(block, block, jax.ShapeDtypeStruct((2, RANK, WIDTH), F32)),
        in_specs=[smem, hbm, hbm, hbm, hbm, hbm, vmem, vmem],
        out_specs=(vmem,) * 3,
        scratch_shapes=[
            pltpu.VMEM((GROUP_HEADS, 4, 2, COLS, HEAD_DIM), BF),
            pltpu.VMEM((GROUP_HEADS, 6, 4, COLS, HEAD_DIM), BF),
            pltpu.VMEM((GROUP_HEADS, 6, 4, COLS, HEAD_DIM), BF),
            pltpu.VMEM((GROUP_HEADS, 4, 2, COLS, HEAD_DIM), BF),
            pltpu.VMEM((8, 2, COLS, WIDTH), BF),
            pltpu.VMEM((2, COLS, WIDTH), BF),
            pltpu.VMEM((2, COLS, WIDTH), BF),
            pltpu.VMEM((2, RANK, WIDTH), BF),
            pltpu.VMEM((7, RANK, GROUP), BF),
            pltpu.VMEM((RANK, GROUP), F32),
            pltpu.VMEM((3, 16, GROUP), F32),
            pltpu.VMEM((16, GROUP), F32),
            pltpu.VMEM((3, 16, GROUP), F32),
            pltpu.VMEM((RANK, GROUP), BF),
            pltpu.VMEM((2, RANK, WIDTH), BF),
            dma((2,)), dma((3, GROUP_HEADS, 4)), dma((3, GROUP_HEADS, 4)),
            dma((2, GROUP_HEADS, 8)), dma((2, GROUP_HEADS, 8)),
            dma((GROUP_HEADS, 4)), dma((GROUP_HEADS, 4)),
            dma((2,)), dma((3,)), dma((3,)), dma((2, 4)), dma((2, 4)), dma((4,)), dma((4,)),
            dma((4, 4)), dma((4, 4)),
            dma((7,)), dma((7,)), dma((3,)), dma((3,)),
            dma((3,)), dma((3,)), dma((3,)), dma((3,)), dma((7,)), dma((7,)),
        ],
        compiler_params=pltpu.CompilerParams(
            collective_id=0, has_side_effects=True, vmem_limit_bytes=56 * 2**20
        ),
        cost_estimate=pl.CostEstimate(
            flops=14_000_000_000, bytes_accessed=100_000_000, transcendentals=7_000_000
        ),
        name="training_step",
    )(
        head_window_radius, queries, keys, values, output_weight,
        output_gradient.reshape(2, COLS, WIDTH), adapter_down_weight, adapter_up_weight,
    )
    shape = (2, 1, COLS, WIDTH)
    return mixed.reshape(shape), back.reshape(shape), grads[0], grads[1].T


def solution(mesh):
    tokens = P("tm", "height", None, None)
    return jax.shard_map(
        per_device,
        mesh=mesh,
        in_specs=(tokens, tokens, tokens, P(), P("height", None), P(), P(), tokens),
        out_specs=(tokens, tokens, P(), P()),
        check_vma=False,
    )
```

```python
import functools
import math

import jax
import jax.numpy as jnp
from jax import lax
from jax.experimental import pallas as pl
from jax.experimental.pallas import tpu as pltpu
from jax.sharding import PartitionSpec as P

HEADS = 20
HEAD_DIM = 128
TILE_W = 16
COLS = 160
HALF = COLS // 2
WINDOW = 128
RANK = 64
ADAPTER_SCALE = 2.0
GRID = 16
CHIPS = 4
GROUP_HEADS = HEADS // CHIPS
GROUP = GROUP_HEADS * HEAD_DIM
WIDTH = HEADS * HEAD_DIM
NEG = -1e30
MESH = pl.DeviceIdType.MESH
BF = jnp.bfloat16
F32 = jnp.float32


def place():
    tm, height = lax.axis_index("tm"), lax.axis_index("height")
    z, xh = tm // 2, tm % 2
    y, xl, core = height // 4, (height // 2) % 2, height % 2
    return z, xh, y, xl, core


def device(z, x, y, core):
    return (z * 2 + x // 2, y * 4 + (x % 2) * 2 + core)


def enter(partners):
    barrier = pltpu.get_barrier_semaphore()
    for partner in partners:
        pl.semaphore_signal(barrier, inc=1, device_id=partner, device_id_type=MESH)
    pl.semaphore_wait(barrier, len(partners))


def remote(src, dst, send, recv, target):
    return pltpu.make_async_remote_copy(
        src_ref=src, dst_ref=dst, send_sem=send, recv_sem=recv, device_id=target, device_id_type=MESH
    )


def arrived(dst, sem):
    pltpu.make_async_copy(dst, dst, sem).wait()


def group_columns(x):
    return pl.ds(pl.multiple_of(x * GROUP, 128), GROUP)


def attend(j, f, half, radii, frame, row_first, q_ref, k_ref, v_ref, o_ref):
    radius_frame, radius_row, radius_column = radii
    start = (COLS - WINDOW) * half
    query_tile = (lax.broadcasted_iota(jnp.int32, (HALF, WINDOW), 0) + half * HALF) // TILE_W
    key_tile = (lax.broadcasted_iota(jnp.int32, (HALF, WINDOW), 1) + start) // TILE_W
    near = jnp.abs(query_tile - key_tile) <= radius_column
    query_rows, key_rows = pl.ds(half * HALF, HALF), pl.ds(start, WINDOW)
    places = [(a, b) for a in range(3) for b in range(4)]
    q = jnp.concatenate([q_ref[j, f, r, query_rows, :] for r in range(2)], axis=0)
    k = jnp.concatenate([k_ref[j, f + a, b, key_rows, :] for a, b in places], axis=0)
    v = jnp.concatenate([v_ref[j, f + a, b, key_rows, :] for a, b in places], axis=0)
    scores = lax.dot_general(q, k, (((1,), (1,)), ((), ())), preferred_element_type=F32)
    scale = math.log2(math.e) / math.sqrt(HEAD_DIM)
    nothing = jnp.zeros((HALF, WINDOW), BF)
    rows = []
    for r in range(2):
        masked = {}
        for at, (a, b) in enumerate(places):
            if not r <= b <= r + 2:
                continue
            s = scores[r * HALF : (r + 1) * HALF, at * WINDOW : (at + 1) * WINDOW]
            allowed = near
            if a != 1 or b != r + 1:
                other_frame, other_row = frame + (a - 1), row_first + (b - 1)
                inside = (
                    (other_frame >= 0) & (other_frame < GRID) & (other_row >= 0) & (other_row < GRID)
                )
                if a != 1:
                    inside = inside & (radius_frame > 0)
                if b != r + 1:
                    inside = inside & (radius_row > 0)
                allowed = near & inside
            masked[a, b] = jnp.where(allowed, s, NEG)
        highest = jnp.max(functools.reduce(jnp.maximum, masked.values()), axis=1, keepdims=True)
        weights = {at: jnp.exp2((s - highest) * scale) for at, s in masked.items()}
        total = jnp.sum(functools.reduce(jnp.add, weights.values()), axis=1, keepdims=True)
        share = 1.0 / total
        rows.append(
            jnp.concatenate(
                [(weights[at] * share).astype(BF) if at in weights else nothing for at in places], axis=1
            )
        )
    result = jnp.dot(jnp.concatenate(rows, axis=0), v, preferred_element_type=F32).astype(BF)
    for r in range(2):
        o_ref[j, f, r, query_rows, :] = result[r * HALF : (r + 1) * HALF]


def step_kernel(
    factor, radius_ref, q_hbm, k_hbm, v_hbm, w_hbm, g_hbm, down_hbm, up_hbm,
    mixed_hbm, back_hbm, grads_hbm,
    mixed_ref, back_ref,
    qs_ref, ks_ref, vs_ref, os_ref, w_ref, g_ref, att_ref,
    part_ref, ra_ref, acc_ref, rb_ref, rd_ref, fin_ref,
    down_ref, up_ref, own_back_ref, back_low_ref, back_turned_ref, down_part_ref, down_got_ref,
    load_sem, out_sem, in_sem, halo_out, halo_in, o_in, p_sem,
    w_out, wx_in, wy_in, wz_in, ws_in, r_sem, e_in, store_sem,
):
    z, xh, y, xl, core = place()
    x = xh * 2 + xl
    here = xl == core
    ring = x * 2 + core
    band = y * 2 + core
    before, after = (band + 7) % 8, (band + 1) % 8
    left = device(z, x, before // 2, before % 2)
    right = device(z, x, after // 2, after % 2)
    sibling = device(z, x, y, 1 - core)

    def ring_device(step):
        other = (ring + step) % 8
        return other // 2, other % 2, device(z, other // 2, y, other % 2)

    def y_device(step):
        return device(z, x, (y + step) % 4, core)

    def z_device(step):
        return device((z + step) % 4, x, y, core)

    up, down = z_device(3), z_device(1)

    def head_columns(chip, j):
        return pl.ds(pl.multiple_of((chip * GROUP_HEADS + j) * HEAD_DIM, HEAD_DIM), HEAD_DIM)

    load_gradient = pltpu.make_async_copy(g_hbm, g_ref, load_sem.at[0])
    load_weight = [
        pltpu.make_async_copy(
            w_hbm.at[:, group_columns((z + quarter) % 4)],
            w_ref.at[y * 2 + xl, core, :, group_columns((z + quarter) % 4)],
            load_sem.at[1 + quarter // 2],
        )
        for quarter in (0, 2)
    ]
    load_up = pltpu.make_async_copy(up_hbm, up_ref, load_sem.at[3])
    load_down = pltpu.make_async_copy(down_hbm, down_ref, load_sem.at[4])
    load_gradient.start()
    load_up.start()
    load_down.start()
    for copy in load_weight:
        copy.start()

    outside = (band + 7 + 2 * core) % 8
    enter(
        [ring_device(step)[2] for step in range(1, 8)]
        + [device((z + step % 4) % 4, x, (y + step // 4) % 4, core) for step in range(1, 16)]
        + [device(z, x, outside // 2, outside % 2)]
    )

    arrays = ((k_hbm, ks_ref, 1), (v_hbm, vs_ref, 1), (q_hbm, qs_ref, 0))

    def exchange(i, j, step):
        src, dst, pad = arrays[i]
        target = (x + step) % CHIPS
        piece = src.at[:, 0, :, head_columns(target, j)]
        slot = dst.at[j, pl.ds(pad + 2 * xh, 2), pad + core]
        return piece, slot, remote(
            piece, slot, out_sem.at[0], in_sem.at[i, j],
            device(z, target, y, xl),
        )

    def give(i, j):
        for step in (2, 1, 3):
            exchange(i, j, step)[2].start()
        piece, slot, copy = exchange(i, j, 0)

        @pl.when(here)
        def _():
            pltpu.make_async_copy(piece, slot, in_sem.at[i, j]).start()

        @pl.when(jnp.logical_not(here))
        def _():
            copy.start()

    def landed(i, j):
        own = (pl.ds(1, 4), pl.ds(1, 2)) if i < 2 else ()
        arrived(arrays[i][1].at[(j, *own)], in_sem.at[i, j])

    def halos(i, j):
        ref = arrays[i][1].at[j]

        def send(n, src, dst, target):
            return remote(src, dst, halo_out.at[i], halo_in.at[i, j, min(n // 2, 1)], target)

        rows, own = pl.ds(1, 2), pl.ds(1, 4)
        return (
            send(0, ref.at[1, rows], ref.at[5, rows], up),
            send(1, ref.at[4, rows], ref.at[0, rows], down),
            send(2, ref.at[own, 1], ref.at[own, 3], left),
            send(3, ref.at[own, 2], ref.at[own, 0], right),
            send(4, ref.at[0, 1], ref.at[0, 3], left),
            send(5, ref.at[5, 1], ref.at[5, 3], left),
            send(6, ref.at[0, 2], ref.at[0, 0], right),
            send(7, ref.at[5, 2], ref.at[5, 0], right),
        )

    def start_halos(j):
        for i in range(2):
            landed(i, j)
            for copy in halos(i, j)[:4]:
                copy.start()

    def start_corners(j):
        for i in range(2):
            arrived(arrays[i][1].at[j, 0], halo_in.at[i, j, 0])
            for copy in halos(i, j)[4:]:
                copy.start()

    def await_head(j):
        for i in range(2):
            arrived(arrays[i][1].at[j, pl.ds(0, 3)], halo_in.at[i, j, 1])
        landed(2, j)

    def attend_frames(j, first, last):
        head = x * GROUP_HEADS + j
        radii = [radius_ref[n, head] for n in range(3)]

        def one(f, carry):
            for half in range(2):
                attend(
                    j, f, half, radii, z * 4 + f, y * 4 + core * 2, qs_ref, ks_ref, vs_ref, os_ref
                )
            return carry

        lax.fori_loop(first, last, one, 0)

    def give_back(j, n):
        frames = (xh + n // 2) % 2
        row = (core + n % 2) % 2
        piece = os_ref.at[j, pl.ds(2 * frames, 2), row]
        slot = att_ref.at[:, :, head_columns(x, j)]
        return piece, slot, remote(
            piece, slot, out_sem.at[1], o_in.at[0], device(z, frames * 2 + core, y, row)
        )

    def start_back(j):
        for n in (2, 3, 1):
            give_back(j, n)[2].start()
        piece, slot, copy = give_back(j, 0)

        @pl.when(here)
        def _():
            pltpu.make_async_copy(piece, slot, o_in.at[0]).start()

        @pl.when(jnp.logical_not(here))
        def _():
            copy.start()

    def weight_piece(quarter, n, side):
        return w_ref.at[pl.ds(2 * ((y + n) % 4), 2), side, :, group_columns((z + quarter) % 4)]

    def weight_shard(quarter, n, part):
        return w_ref.at[
            2 * ((y + n) % 4) + (xl + part) % 2, core, :, group_columns((z + quarter) % 4)
        ]

    def weight_x(quarter):
        piece = weight_shard(quarter, 0, 0)
        other = (xh + quarter // 2) % 2 * 2 + 1 - xl
        return remote(
            piece, piece, w_out.at[0], wx_in.at[quarter // 2],
            device(z, other, y, core),
        )

    def weight_y(quarter, step, part):
        piece = weight_shard(quarter, 0, part)
        at = quarter // 2
        return remote(
            piece, piece, w_out.at[1], wy_in.at[at, 3 - step],
            y_device(step),
        )

    def weight_z_shard(way, part):
        piece = weight_shard(0, 0, part)
        return remote(piece, piece, w_out.at[2], wz_in.at[way, 0], (up, down)[way])

    def weight_z(way, n):
        piece = weight_piece(0, n, core)
        return remote(piece, piece, w_out.at[2], wz_in.at[way, n], (up, down)[way])

    def weight_sibling(quarter, n):
        piece = weight_piece(quarter, n, core)
        return remote(piece, piece, w_out.at[3], ws_in.at[0], sibling)

    def start_y(quarter, part, steps=(1, 3, 2)):
        for step in steps:
            weight_y(quarter, step, part).start()

    def start_z_shard(part):
        for way in range(2):
            weight_z_shard(way, part).start()

    def take_y(quarter, n):
        arrived(weight_piece(quarter, n, core), wy_in.at[quarter // 2, n - 1])
        weight_sibling(quarter, n).start()

    def spread_weight(n):
        take_y(0, n)
        weight_z(0, n).start()
        weight_z(1, n).start()

    def take_z(n):
        for way, quarter in ((0, 1), (1, 3)):
            arrived(weight_piece(quarter, n, core), wz_in.at[way, n])
            weight_sibling(quarter, n).start()

    def give_low(step):
        target = (x + step) % CHIPS
        return remote(
            own_back_ref, back_low_ref.at[xh, core], out_sem.at[2], o_in.at[1],
            device(z, target, y, xl),
        )

    def add_down(j):
        total = jnp.zeros((RANK, HEAD_DIM), F32)
        for f in range(4):
            for r in range(2):
                total = total + jnp.dot(
                    back_turned_ref[f, r], os_ref[j, f, r], preferred_element_type=F32
                )
        down_part_ref[:, j * HEAD_DIM : (j + 1) * HEAD_DIM] = factor * total

    def half_rows(n):
        return pl.ds(pl.multiple_of(n * 32, 32), 32)

    down_to_sibling = remote(
        down_part_ref.at[half_rows(1 - core)], down_got_ref, p_sem.at[0], p_sem.at[1], sibling
    )

    K, V, Q = 0, 1, 2
    for copy in load_weight:
        copy.wait()
    weight_x(0).start()
    start_y(0, 0)
    start_z_shard(0)
    give(K, 0)
    give(V, 0)
    weight_x(2).start()
    load_gradient.wait()
    load_up.wait()
    load_down.wait()
    contract_last = (((1,), (1,)), ((), ()))
    contract_first = (((0,), (0,)), ((), ()))
    tokens = 2 * COLS
    low_back = lax.dot_general(
        g_ref[...].reshape(tokens, WIDTH), up_ref[...], contract_last, preferred_element_type=F32
    ).astype(BF)
    own_back_ref[...] = jnp.concatenate([low_back[:COLS], low_back[COLS:]], axis=1)
    for step in (2, 1, 3):
        give_low(step).start()
    low_copy = give_low(0)
    low_slot = back_low_ref.at[xh, core]

    @pl.when(here)
    def _():
        pltpu.make_async_copy(own_back_ref, low_slot, o_in.at[1]).start()

    @pl.when(jnp.logical_not(here))
    def _():
        low_copy.start()

    for i, j in (
        (K, 1), (V, 1), (Q, 0), (K, 2), (V, 2), (Q, 1),
        (K, 3), (V, 3), (Q, 2), (K, 4), (V, 4), (Q, 3), (Q, 4),
    ):
        give(i, j)
    weight_x(0).wait_recv()
    start_y(0, 1)
    start_z_shard(1)
    weight_sibling(0, 0).start()

    start_halos(0)
    start_corners(0)
    spread_weight(1)
    start_halos(1)
    arrived(back_low_ref, o_in.at[1])
    for pair in range(2):
        for row in range(2):
            turned = back_low_ref[pair, row].astype(F32).T.astype(BF)
            for n in range(2):
                frame = 2 * pair + n
                back_turned_ref[frame, row] = turned[n * RANK : (n + 1) * RANK]
    await_head(0)
    weight_x(2).wait_recv()
    start_y(2, 0, (1, 3))
    weight_sibling(2, 0).start()
    attend_frames(0, 0, 4)
    start_back(0)
    add_down(0)
    start_corners(1)

    start_halos(2)
    await_head(1)
    start_y(2, 0, (2,))
    spread_weight(3)
    take_z(0)
    attend_frames(1, 0, 4)
    start_back(1)
    add_down(1)
    start_corners(2)

    start_halos(3)
    await_head(2)
    start_y(2, 1, (1, 3))
    spread_weight(2)
    take_z(1)
    attend_frames(2, 0, 4)
    start_back(2)
    add_down(2)
    start_corners(3)

    start_halos(4)
    await_head(3)
    start_y(2, 1, (2,))
    take_z(3)
    attend_frames(3, 0, 2)
    start_corners(4)
    attend_frames(3, 2, 4)
    start_back(3)
    add_down(3)
    for n in range(1, 4):
        take_y(2, n)
    take_z(2)
    await_head(4)
    attend_frames(4, 0, 4)
    start_back(4)
    add_down(4)
    down_to_sibling.start()

    step_width = 256

    def forward(j, carry):
        columns = pl.ds(pl.multiple_of(j * step_width, step_width), step_width)
        frozen = jnp.dot(
            att_ref[...].reshape(tokens, WIDTH), w_ref[:, :, :, columns].reshape(WIDTH, step_width),
            preferred_element_type=F32,
        )
        adapter = jnp.dot(low, up_ref[:, columns], preferred_element_type=F32)
        mixed_ref[:, :, columns] = (
            (frozen + ADAPTER_SCALE * adapter).astype(BF).reshape(2, COLS, step_width)
        )
        return carry

    def backward(j, carry):
        rows = group_columns(j)
        frozen = lax.dot_general(
            g_ref[...].reshape(tokens, WIDTH), w_ref[pl.ds(2 * j, 2)].reshape(GROUP, WIDTH),
            contract_last, preferred_element_type=F32,
        )
        adapter = jnp.dot(low_back, down_ref[:, rows], preferred_element_type=F32)
        back_ref[:, :, rows] = (
            (frozen + ADAPTER_SCALE * adapter).astype(BF).reshape(2, COLS, GROUP)
        )
        return carry

    arrived(w_ref.at[:, 1 - core], ws_in.at[0])
    lax.fori_loop(0, CHIPS, backward, 0)
    store_back = pltpu.make_async_copy(back_ref, back_hbm, store_sem.at[0])
    store_back.start()

    arrived(att_ref, o_in.at[0])
    low = lax.dot_general(
        att_ref[...].reshape(tokens, WIDTH), down_ref[...], contract_last, preferred_element_type=F32
    ).astype(BF)
    part_ref[...] = (
        factor
        * lax.dot_general(
            low, g_ref[...].reshape(tokens, WIDTH), contract_first, preferred_element_type=F32
        )
    ).astype(BF)

    def phase_a(step):
        tx, tc, target = ring_device(step)
        return remote(
            part_ref.at[half_rows(tc), group_columns(tx)], ra_ref.at[step - 1],
            r_sem.at[0], r_sem.at[1], target,
        )

    for step in range(1, 8):
        phase_a(step).start()

    blocks = WIDTH // step_width
    lax.fori_loop(0, blocks // 2, forward, 0)
    @pl.when(here)
    def _():
        arrived(ks_ref.at[:, :, pl.ds(0, 3)], out_sem.at[0])
        arrived(qs_ref.at[:, pl.ds(0, 3)], out_sem.at[1])
        arrived(ks_ref.at[0, 0, pl.ds(0, 3)], out_sem.at[2])

    @pl.when(jnp.logical_not(here))
    def _():
        arrived(ks_ref, out_sem.at[0])
        arrived(qs_ref, out_sem.at[1])
        arrived(back_low_ref, out_sem.at[2])

    for i in range(2):
        arrived(arrays[i][1].at[:, pl.ds(0, 4)], halo_out.at[i])
    arrived(w_ref.at[0, :, :, pl.ds(0, GROUP)], w_out.at[0])
    arrived(w_ref.at[pl.ds(0, 6), :, :, pl.ds(0, GROUP)], w_out.at[1])
    arrived(w_ref.at[:, :, :, pl.ds(0, GROUP)], w_out.at[2])
    arrived(w_ref.at[:, :, :, pl.ds(0, 2 * GROUP)], w_out.at[3])
    down_to_sibling.wait_send()
    down_to_sibling.wait_recv()
    acc_ref[2:] = (
        (down_part_ref[half_rows(core), :] + down_got_ref[...]).astype(BF).reshape(2, 16, GROUP)
    )
    total = part_ref[half_rows(core), group_columns(x)].astype(F32)
    arrived(ra_ref, r_sem.at[1])
    for step in range(1, 8):
        total = total + ra_ref[step - 1].astype(F32)
    acc_ref[:2] = total.astype(BF).reshape(2, 16, GROUP)

    def phase_b(step):
        dy, dz = step // 4, step % 4
        return remote(
            acc_ref.at[(y + dy) % 4], rb_ref.at[y * 4 + z], r_sem.at[2], r_sem.at[3],
            device((z + dz) % 4, x, (y + dy) % 4, core),
        )

    for step in range(1, 16):
        phase_b(step).start()
    rb_ref[y * 4 + z] = acc_ref[y]
    lax.fori_loop(blocks // 2, blocks, forward, 0)
    store_mixed = pltpu.make_async_copy(mixed_ref, mixed_hbm, store_sem.at[1])
    store_mixed.start()
    arrived(rb_ref.at[pl.ds(0, 15)], r_sem.at[3])
    total = rb_ref[0].astype(F32)
    for source in range(1, 16):
        total = total + rb_ref[source].astype(F32)
    rd_ref[y // 2, y % 2] = total.astype(BF)

    def phase_d(step):
        return remote(
            rd_ref.at[y // 2, y % 2], rd_ref.at[y // 2, y % 2],
            r_sem.at[4], r_sem.at[5], y_device(step),
        )

    for step in range(1, 4):
        phase_d(step).start()
    arrived(rb_ref.at[pl.ds(0, 3)], r_sem.at[5])

    def share(tx, tc):
        return fin_ref.at[:, pl.ds(2 * tc, 2), :, group_columns(tx)]

    def phase_e(step):
        return remote(
            rd_ref, share(x, core), r_sem.at[6], e_in.at[step],
            device(z, (x + step) % CHIPS, y, core),
        )

    def pass_share(step):
        piece = share((x + CHIPS - step) % CHIPS, core)
        return remote(piece, piece, r_sem.at[7], e_in.at[0], sibling)

    for step in (2, 1, 3):
        phase_e(step).start()
    fin_ref[:, pl.ds(2 * core, 2), :, group_columns(x)] = rd_ref[...]
    pass_share(0).start()
    for step in (1, 3, 2):
        arrived(share((x + CHIPS - step) % CHIPS, core), e_in.at[step])
        pass_share(step).start()
    arrived(fin_ref.at[:, pl.ds(2 * (1 - core), 2)], e_in.at[0])
    store_grads = pltpu.make_async_copy(fin_ref, grads_hbm, store_sem.at[2])
    store_grads.start()
    arrived(ra_ref, r_sem.at[0])
    arrived(rb_ref.at[pl.ds(0, 15)], r_sem.at[2])
    arrived(rb_ref.at[pl.ds(0, 3)], r_sem.at[4])
    arrived(rb_ref.at[pl.ds(0, 12)], r_sem.at[6])
    arrived(rb_ref, r_sem.at[7])
    store_back.wait()
    store_mixed.wait()
    store_grads.wait()


def deliver_kernel(
    mixed_hbm, back_hbm, grads_hbm, mixed_out, back_out, grad_up_out, grad_down_out,
    held_ref, grads_ref, wide_ref, take_sem, put_sem,
):
    takes = [pltpu.make_async_copy(grads_hbm, grads_ref, take_sem.at[0])]
    puts = []
    for f in range(2):
        for n, (src, dst) in enumerate(((mixed_hbm, mixed_out), (back_hbm, back_out))):
            at = 1 + 2 * f + n
            takes.append(pltpu.make_async_copy(src.at[f], held_ref.at[n, f], take_sem.at[at]))
            puts.append(pltpu.make_async_copy(held_ref.at[n, f], dst.at[f], put_sem.at[at]))
    for copy in takes:
        copy.start()
    for n, dst in enumerate((grad_up_out, grad_down_out)):
        if n == 0:
            takes[0].wait()
        wide_ref[n] = grads_ref[n].astype(F32).reshape(RANK, WIDTH)
        copy = pltpu.make_async_copy(wide_ref.at[n], dst, put_sem.at[5 * n])
        copy.start()
        puts.append(copy)
    for take, put in zip(takes[1:], puts[:4]):
        take.wait()
        put.start()
    for copy in puts:
        copy.wait()


def per_device(
    queries, keys, values, head_window_radius, output_weight, adapter_down_weight, adapter_up_weight,
    output_gradient,
):
    factor = ADAPTER_SCALE / math.sqrt(GRID * GRID * COLS)
    smem = pl.BlockSpec(memory_space=pltpu.SMEM)
    hbm = pl.BlockSpec(memory_space=pl.ANY)
    block = jax.ShapeDtypeStruct((2, COLS, WIDTH), BF)
    dma = pltpu.SemaphoreType.DMA
    small = jax.ShapeDtypeStruct((RANK, WIDTH), F32)
    mixed, back, grads = pl.pallas_call(
        functools.partial(step_kernel, factor),
        out_shape=(block, block, jax.ShapeDtypeStruct((2, 4, 16, WIDTH), BF)),
        in_specs=[smem, hbm, hbm, hbm, hbm, hbm, hbm, hbm],
        out_specs=(hbm,) * 3,
        scratch_shapes=[
            pltpu.VMEM((2, COLS, WIDTH), BF),
            pltpu.VMEM((2, COLS, WIDTH), BF),
            pltpu.VMEM((GROUP_HEADS, 4, 2, COLS, HEAD_DIM), BF),
            pltpu.VMEM((GROUP_HEADS, 6, 4, COLS, HEAD_DIM), BF),
            pltpu.VMEM((GROUP_HEADS, 6, 4, COLS, HEAD_DIM), BF),
            pltpu.VMEM((GROUP_HEADS, 4, 2, COLS, HEAD_DIM), BF),
            pltpu.VMEM((8, 2, COLS, WIDTH), BF),
            pltpu.VMEM((2, COLS, WIDTH), BF),
            pltpu.VMEM((2, COLS, WIDTH), BF),
            pltpu.VMEM((RANK, WIDTH), BF),
            pltpu.VMEM((7, 32, GROUP), BF),
            pltpu.VMEM((4, 16, GROUP), BF),
            pltpu.VMEM((16, 16, GROUP), BF),
            pltpu.VMEM((2, 2, 16, GROUP), BF),
            pltpu.VMEM((2, 4, 16, WIDTH), BF),
            pltpu.VMEM((RANK, WIDTH), BF),
            pltpu.VMEM((RANK, WIDTH), BF),
            pltpu.VMEM((COLS, 2 * RANK), BF),
            pltpu.VMEM((2, 2, COLS, 2 * RANK), BF),
            pltpu.VMEM((4, 2, RANK, COLS), BF),
            pltpu.VMEM((RANK, GROUP), F32),
            pltpu.VMEM((32, GROUP), F32),
            dma((5,)), dma((3,)), dma((3, GROUP_HEADS)), dma((2,)), dma((2, GROUP_HEADS, 2)),
            dma((2,)), dma((2,)),
            dma((4,)), dma((2,)), dma((2, 3)), dma((2, 4)), dma((1,)), dma((8,)), dma((4,)), dma((3,)),
        ],
        compiler_params=pltpu.CompilerParams(
            collective_id=0, has_side_effects=True, vmem_limit_bytes=57 * 2**20
        ),
        cost_estimate=pl.CostEstimate(
            flops=14_000_000_000, bytes_accessed=100_000_000, transcendentals=7_000_000
        ),
        name="training_step",
    )(
        head_window_radius.T, queries, keys, values, output_weight,
        output_gradient.reshape(2, COLS, WIDTH), adapter_down_weight.T, adapter_up_weight,
    )
    mixed, back, grad_up, grad_down = pl.pallas_call(
        deliver_kernel,
        out_shape=(block, block, small, small),
        in_specs=[hbm] * 3,
        out_specs=(hbm,) * 4,
        scratch_shapes=[
            pltpu.VMEM((2, 2, COLS, WIDTH), BF),
            pltpu.VMEM((2, 4, 16, WIDTH), BF),
            pltpu.VMEM((2, RANK, WIDTH), F32),
            dma((5,)),
            dma((6,)),
        ],
        compiler_params=pltpu.CompilerParams(vmem_limit_bytes=60 * 2**20),
        name="deliver",
    )(mixed, back, grads)
    shape = (2, 1, COLS, WIDTH)
    return mixed.reshape(shape), back.reshape(shape), grad_up, grad_down.T


def solution(mesh):
    tokens = P("tm", "height", None, None)
    return jax.shard_map(
        per_device,
        mesh=mesh,
        in_specs=(tokens, tokens, tokens, P(), P("height", None), P(), P(), tokens),
        out_specs=(tokens, tokens, P(), P()),
        check_vma=False,
    )
```

```python
import functools
import math

import jax
import jax.numpy as jnp
from jax import lax
from jax.experimental import pallas as pl
from jax.experimental.pallas import tpu as pltpu
from jax.sharding import PartitionSpec as P

HEADS = 20
HEAD_DIM = 128
TILE_W = 16
COLS = 160
HALF = COLS // 2
WINDOW = 128
RANK = 64
ADAPTER_SCALE = 2.0
GRID = 16
CHIPS = 4
GROUP_HEADS = HEADS // CHIPS
GROUP = GROUP_HEADS * HEAD_DIM
WIDTH = HEADS * HEAD_DIM
NEG = -1e30
MESH = pl.DeviceIdType.MESH
BF = jnp.bfloat16
F32 = jnp.float32


def place():
    tm, height = lax.axis_index("tm"), lax.axis_index("height")
    z, xh = tm // 2, tm % 2
    y, xl, core = height // 4, (height // 2) % 2, height % 2
    return z, xh, y, xl, core


def device(z, x, y, core):
    return (z * 2 + x // 2, y * 4 + (x % 2) * 2 + core)


def enter(partners):
    barrier = pltpu.get_barrier_semaphore()
    for partner in partners:
        pl.semaphore_signal(barrier, inc=1, device_id=partner, device_id_type=MESH)
    pl.semaphore_wait(barrier, len(partners))


def remote(src, dst, send, recv, target):
    return pltpu.make_async_remote_copy(
        src_ref=src, dst_ref=dst, send_sem=send, recv_sem=recv, device_id=target, device_id_type=MESH
    )


def arrived(dst, sem):
    pltpu.make_async_copy(dst, dst, sem).wait()


def group_columns(x):
    return pl.ds(pl.multiple_of(x * GROUP, 128), GROUP)


def attend(j, f, half, radii, frame, row_first, q_ref, k_ref, v_ref, o_ref):
    radius_frame, radius_row, radius_column = radii
    start = (COLS - WINDOW) * half
    query_tile = (lax.broadcasted_iota(jnp.int32, (HALF, WINDOW), 0) + half * HALF) // TILE_W
    key_tile = (lax.broadcasted_iota(jnp.int32, (HALF, WINDOW), 1) + start) // TILE_W
    near = jnp.abs(query_tile - key_tile) <= radius_column
    query_rows, key_rows = pl.ds(half * HALF, HALF), pl.ds(start, WINDOW)
    places = [(a, b) for a in range(3) for b in range(4)]
    q = jnp.concatenate([q_ref[j, f, r, query_rows, :] for r in range(2)], axis=0)
    k = jnp.concatenate([k_ref[j, f + a, b, key_rows, :] for a, b in places], axis=0)
    v = jnp.concatenate([v_ref[j, f + a, b, key_rows, :] for a, b in places], axis=0)
    scores = lax.dot_general(q, k, (((1,), (1,)), ((), ())), preferred_element_type=F32)
    scale = math.log2(math.e) / math.sqrt(HEAD_DIM)
    nothing = jnp.zeros((HALF, WINDOW), BF)
    rows = []
    for r in range(2):
        masked = {}
        for at, (a, b) in enumerate(places):
            if not r <= b <= r + 2:
                continue
            s = scores[r * HALF : (r + 1) * HALF, at * WINDOW : (at + 1) * WINDOW]
            allowed = near
            if a != 1 or b != r + 1:
                other_frame, other_row = frame + (a - 1), row_first + (b - 1)
                inside = (
                    (other_frame >= 0) & (other_frame < GRID) & (other_row >= 0) & (other_row < GRID)
                )
                if a != 1:
                    inside = inside & (radius_frame > 0)
                if b != r + 1:
                    inside = inside & (radius_row > 0)
                allowed = near & inside
            masked[a, b] = jnp.where(allowed, s, NEG)
        highest = jnp.max(functools.reduce(jnp.maximum, masked.values()), axis=1, keepdims=True)
        weights = {at: jnp.exp2((s - highest) * scale) for at, s in masked.items()}
        total = jnp.sum(functools.reduce(jnp.add, weights.values()), axis=1, keepdims=True)
        share = 1.0 / total
        rows.append(
            jnp.concatenate(
                [(weights[at] * share).astype(BF) if at in weights else nothing for at in places], axis=1
            )
        )
    result = jnp.dot(jnp.concatenate(rows, axis=0), v, preferred_element_type=F32).astype(BF)
    for r in range(2):
        o_ref[j, f, r, query_rows, :] = result[r * HALF : (r + 1) * HALF]


def step_kernel(
    factor, radius_ref, q_hbm, k_hbm, v_hbm, w_hbm, g_hbm, down_hbm, up_hbm,
    mixed_hbm, back_hbm, grads_hbm,
    mixed_ref, back_ref,
    qs_ref, ks_ref, vs_ref, os_ref, w_ref, g_ref, att_ref,
    part_ref, ra_ref, acc_ref, rb_ref, rd_ref, rounded_ref, fin_ref,
    down_ref, up_ref, own_back_ref, back_low_ref, back_turned_ref, down_part_ref, down_got_ref,
    load_sem, out_sem, in_sem, halo_out, halo_in, o_in, p_sem,
    w_out, wx_in, wy_in, wz_in, ws_in, r_sem, e_in, store_sem,
):
    z, xh, y, xl, core = place()
    x = xh * 2 + xl
    here = xl == core
    ring = x * 2 + core
    band = y * 2 + core
    before, after = (band + 7) % 8, (band + 1) % 8
    left = device(z, x, before // 2, before % 2)
    right = device(z, x, after // 2, after % 2)
    sibling = device(z, x, y, 1 - core)

    def ring_device(step):
        other = (ring + step) % 8
        return other // 2, other % 2, device(z, other // 2, y, other % 2)

    def y_device(step):
        return device(z, x, (y + step) % 4, core)

    def z_device(step):
        return device((z + step) % 4, x, y, core)

    up, down = z_device(3), z_device(1)

    def head_columns(chip, j):
        return pl.ds(pl.multiple_of((chip * GROUP_HEADS + j) * HEAD_DIM, HEAD_DIM), HEAD_DIM)

    load_gradient = pltpu.make_async_copy(g_hbm, g_ref, load_sem.at[0])
    load_weight = [
        pltpu.make_async_copy(
            w_hbm.at[:, group_columns((z + quarter) % 4)],
            w_ref.at[y * 2 + xl, core, :, group_columns((z + quarter) % 4)],
            load_sem.at[1 + quarter // 2],
        )
        for quarter in (0, 2)
    ]
    load_up = pltpu.make_async_copy(up_hbm, up_ref, load_sem.at[3])
    load_down = pltpu.make_async_copy(down_hbm, down_ref, load_sem.at[4])
    load_gradient.start()
    load_up.start()
    load_down.start()
    for copy in load_weight:
        copy.start()

    outside = (band + 7 + 2 * core) % 8
    enter(
        [ring_device(step)[2] for step in range(1, 8)]
        + [device((z + step % 4) % 4, x, (y + step // 4) % 4, core) for step in range(1, 16)]
        + [device(z, x, outside // 2, outside % 2)]
    )

    arrays = ((k_hbm, ks_ref, 1), (v_hbm, vs_ref, 1), (q_hbm, qs_ref, 0))

    def exchange(i, j, step):
        src, dst, pad = arrays[i]
        target = (x + step) % CHIPS
        piece = src.at[:, 0, :, head_columns(target, j)]
        slot = dst.at[j, pl.ds(pad + 2 * xh, 2), pad + core]
        return piece, slot, remote(
            piece, slot, out_sem.at[0], in_sem.at[i, j],
            device(z, target, y, xl),
        )

    def give(i, j):
        for step in (2, 1, 3):
            exchange(i, j, step)[2].start()
        piece, slot, copy = exchange(i, j, 0)

        @pl.when(here)
        def _():
            pltpu.make_async_copy(piece, slot, in_sem.at[i, j]).start()

        @pl.when(jnp.logical_not(here))
        def _():
            copy.start()

    def landed(i, j):
        own = (pl.ds(1, 4), pl.ds(1, 2)) if i < 2 else ()
        arrived(arrays[i][1].at[(j, *own)], in_sem.at[i, j])

    def halos(i, j):
        ref = arrays[i][1].at[j]

        def send(n, src, dst, target):
            return remote(src, dst, halo_out.at[i], halo_in.at[i, j, min(n // 2, 1)], target)

        rows, own = pl.ds(1, 2), pl.ds(1, 4)
        return (
            send(0, ref.at[1, rows], ref.at[5, rows], up),
            send(1, ref.at[4, rows], ref.at[0, rows], down),
            send(2, ref.at[own, 1], ref.at[own, 3], left),
            send(3, ref.at[own, 2], ref.at[own, 0], right),
            send(4, ref.at[0, 1], ref.at[0, 3], left),
            send(5, ref.at[5, 1], ref.at[5, 3], left),
            send(6, ref.at[0, 2], ref.at[0, 0], right),
            send(7, ref.at[5, 2], ref.at[5, 0], right),
        )

    def start_halos(j):
        for i in range(2):
            landed(i, j)
            for copy in halos(i, j)[:4]:
                copy.start()

    def start_corners(j):
        for i in range(2):
            arrived(arrays[i][1].at[j, 0], halo_in.at[i, j, 0])
            for copy in halos(i, j)[4:]:
                copy.start()

    def await_head(j):
        for i in range(2):
            arrived(arrays[i][1].at[j, pl.ds(0, 3)], halo_in.at[i, j, 1])
        landed(2, j)

    def attend_frames(j, first, last):
        head = x * GROUP_HEADS + j
        radii = [radius_ref[n, head] for n in range(3)]

        def one(f, carry):
            for half in range(2):
                attend(
                    j, f, half, radii, z * 4 + f, y * 4 + core * 2, qs_ref, ks_ref, vs_ref, os_ref
                )
            return carry

        lax.fori_loop(first, last, one, 0)

    def give_back(j, n):
        frames = (xh + n // 2) % 2
        row = (core + n % 2) % 2
        piece = os_ref.at[j, pl.ds(2 * frames, 2), row]
        slot = att_ref.at[:, :, head_columns(x, j)]
        return piece, slot, remote(
            piece, slot, out_sem.at[1], o_in.at[0], device(z, frames * 2 + core, y, row)
        )

    def start_back(j, near=True, far=True):
        if far:
            give_back(j, 2)[2].start()
            give_back(j, 3)[2].start()
        if not near:
            return
        give_back(j, 1)[2].start()
        piece, slot, copy = give_back(j, 0)

        @pl.when(here)
        def _():
            pltpu.make_async_copy(piece, slot, o_in.at[0]).start()

        @pl.when(jnp.logical_not(here))
        def _():
            copy.start()

    def weight_piece(quarter, n, side):
        return w_ref.at[pl.ds(2 * ((y + n) % 4), 2), side, :, group_columns((z + quarter) % 4)]

    def weight_shard(quarter, n, part):
        return w_ref.at[
            2 * ((y + n) % 4) + (xl + part) % 2, core, :, group_columns((z + quarter) % 4)
        ]

    def weight_x(quarter):
        piece = weight_shard(quarter, 0, 0)
        other = (xh + quarter // 2) % 2 * 2 + 1 - xl
        return remote(
            piece, piece, w_out.at[0], wx_in.at[quarter // 2],
            device(z, other, y, core),
        )

    def weight_y(quarter, step, part):
        piece = weight_shard(quarter, 0, part)
        at = quarter // 2
        return remote(
            piece, piece, w_out.at[1], wy_in.at[at, 3 - step],
            y_device(step),
        )

    def weight_z_shard(way, part):
        piece = weight_shard(0, 0, part)
        return remote(piece, piece, w_out.at[2], wz_in.at[way, 0], (up, down)[way])

    def weight_z(way, n):
        piece = weight_piece(0, n, core)
        return remote(piece, piece, w_out.at[2], wz_in.at[way, n], (up, down)[way])

    def weight_sibling(quarter, n):
        piece = weight_piece(quarter, n, core)
        return remote(piece, piece, w_out.at[3], ws_in.at[0], sibling)

    def start_y(quarter, part, steps=(1, 3, 2)):
        for step in steps:
            weight_y(quarter, step, part).start()

    def start_z_shard(part):
        for way in range(2):
            weight_z_shard(way, part).start()

    def take_y(quarter, n):
        arrived(weight_piece(quarter, n, core), wy_in.at[quarter // 2, n - 1])
        weight_sibling(quarter, n).start()

    def spread_weight(n):
        take_y(0, n)
        weight_z(0, n).start()
        weight_z(1, n).start()

    def take_z(n):
        for way, quarter in ((0, 1), (1, 3)):
            arrived(weight_piece(quarter, n, core), wz_in.at[way, n])
            weight_sibling(quarter, n).start()

    def give_low(step):
        target = (x + step) % CHIPS
        return remote(
            own_back_ref, back_low_ref.at[xh, core], out_sem.at[2], o_in.at[1],
            device(z, target, y, xl),
        )

    def add_down(j):
        total = jnp.zeros((RANK, HEAD_DIM), F32)
        for f in range(4):
            for r in range(2):
                total = total + jnp.dot(
                    back_turned_ref[f, r], os_ref[j, f, r], preferred_element_type=F32
                )
        down_part_ref[:, j * HEAD_DIM : (j + 1) * HEAD_DIM] = factor * total

    def half_rows(n):
        return pl.ds(pl.multiple_of(n * 32, 32), 32)

    down_to_sibling = remote(
        down_part_ref.at[half_rows(1 - core)], down_got_ref, p_sem.at[0], p_sem.at[1], sibling
    )

    def start_sum(a):
        for step in range(1, 16):
            sum_copy(a, step).start()
        rb_ref[a, y * 4 + z] = acc_ref[a, y]

    def sum_copy(a, step):
        dy, dz = step // 4, step % 4
        return remote(
            acc_ref.at[a, (y + dy) % 4], rb_ref.at[a, y * 4 + z], r_sem.at[a, 0], r_sem.at[a, 1],
            device((z + dz) % 4, x, (y + dy) % 4, core),
        )

    def round_y(a, step):
        return remote(
            rd_ref.at[a, y], rd_ref.at[a, y], r_sem.at[a, 2], r_sem.at[a, 3], y_device(step)
        )

    def finish_sum(a):
        arrived(rb_ref.at[a, pl.ds(0, 15)], r_sem.at[a, 1])
        total = rb_ref[a, 0]
        for source in range(1, 16):
            total = total + rb_ref[a, source]
        rd_ref[a, y] = total
        for step in range(1, 4):
            round_y(a, step).start()

    def share(a, tx, tc):
        return fin_ref.at[a, half_rows(tc), group_columns(tx)]

    def round_x(a, step):
        return remote(
            rounded_ref.at[a], share(a, x, core), r_sem.at[a, 4], e_in.at[a, step],
            device(z, (x + step) % CHIPS, y, core),
        )

    def pass_share(a, step):
        piece = share(a, (x + CHIPS - step) % CHIPS, core)
        return remote(piece, piece, r_sem.at[a, 5], e_in.at[a, 0], sibling)

    def start_round(a):
        arrived(rb_ref.at[a, pl.ds(0, 3)], r_sem.at[a, 3])
        rounded_ref[a] = rd_ref[a].reshape(32, GROUP).astype(BF)
        for step in (2, 1, 3):
            round_x(a, step).start()
        fin_ref[a, half_rows(core), group_columns(x)] = rounded_ref[a]
        pass_share(a, 0).start()

    def pass_round(a):
        for step in (1, 3, 2):
            arrived(share(a, (x + CHIPS - step) % CHIPS, core), e_in.at[a, step])
            pass_share(a, step).start()

    def finish_round(a):
        arrived(fin_ref.at[a, half_rows(1 - core)], e_in.at[a, 0])
        arrived(rb_ref.at[a, pl.ds(0, 15)], r_sem.at[a, 0])
        arrived(rb_ref.at[a, pl.ds(0, 3)], r_sem.at[a, 2])
        arrived(fin_ref.at[a, pl.ds(0, 32), pl.ds(0, 3 * GROUP)], r_sem.at[a, 4])
        arrived(fin_ref.at[a, pl.ds(0, 32)], r_sem.at[a, 5])

    K, V, Q = 0, 1, 2
    for copy in load_weight:
        copy.wait()
    weight_x(0).start()
    start_y(0, 0)
    start_z_shard(0)
    give(K, 0)
    give(V, 0)
    weight_x(2).start()
    load_gradient.wait()
    load_up.wait()
    load_down.wait()
    contract_last = (((1,), (1,)), ((), ()))
    contract_first = (((0,), (0,)), ((), ()))
    tokens = 2 * COLS
    low_back = lax.dot_general(
        g_ref[...].reshape(tokens, WIDTH), up_ref[...], contract_last, preferred_element_type=F32
    ).astype(BF)
    own_back_ref[...] = jnp.concatenate([low_back[:COLS], low_back[COLS:]], axis=1)
    for step in (2, 1, 3):
        give_low(step).start()
    low_copy = give_low(0)
    low_slot = back_low_ref.at[xh, core]

    @pl.when(here)
    def _():
        pltpu.make_async_copy(own_back_ref, low_slot, o_in.at[1]).start()

    @pl.when(jnp.logical_not(here))
    def _():
        low_copy.start()

    for i, j in (
        (K, 1), (V, 1), (Q, 0), (K, 2), (V, 2), (Q, 1),
        (K, 3), (V, 3), (Q, 2), (K, 4), (V, 4), (Q, 3), (Q, 4),
    ):
        give(i, j)
    weight_x(0).wait_recv()
    start_y(0, 1)
    start_z_shard(1)
    weight_sibling(0, 0).start()

    start_halos(0)
    start_corners(0)
    spread_weight(1)
    start_halos(1)
    arrived(back_low_ref, o_in.at[1])
    for pair in range(2):
        for row in range(2):
            turned = back_low_ref[pair, row].astype(F32).T.astype(BF)
            for n in range(2):
                frame = 2 * pair + n
                back_turned_ref[frame, row] = turned[n * RANK : (n + 1) * RANK]
    await_head(0)
    spread_weight(3)
    weight_x(2).wait_recv()
    start_y(2, 0, (1, 3))
    weight_sibling(2, 0).start()
    attend_frames(0, 0, 4)
    start_back(0)
    add_down(0)
    start_corners(1)

    start_halos(2)
    await_head(1)
    start_y(2, 0, (2,))
    spread_weight(2)
    take_z(0)
    attend_frames(1, 0, 4)
    start_back(1)
    add_down(1)
    start_corners(2)

    start_halos(3)
    await_head(2)
    start_y(2, 1, (1, 3))
    take_z(1)
    attend_frames(2, 0, 4)
    start_back(2)
    add_down(2)
    start_corners(3)

    start_halos(4)
    await_head(3)
    start_y(2, 1, (2,))
    take_z(3)
    attend_frames(3, 0, 2)
    start_corners(4)
    attend_frames(3, 2, 4)
    start_back(3)
    add_down(3)
    for n in range(1, 4):
        take_y(2, n)
    take_z(2)
    await_head(4)
    far_frames = 2 * (1 - xh)
    attend_frames(4, far_frames, far_frames + 2)
    start_back(4, near=False)
    attend_frames(4, 2 - far_frames, 4 - far_frames)
    start_back(4, far=False)
    add_down(4)
    down_to_sibling.start()

    step_width = 256

    def forward(j, carry):
        columns = pl.ds(pl.multiple_of(j * step_width, step_width), step_width)
        frozen = jnp.dot(
            att_ref[...].reshape(tokens, WIDTH), w_ref[:, :, :, columns].reshape(WIDTH, step_width),
            preferred_element_type=F32,
        )
        adapter = jnp.dot(low, up_ref[:, columns], preferred_element_type=F32)
        mixed_ref[:, :, columns] = (
            (frozen + ADAPTER_SCALE * adapter).astype(BF).reshape(2, COLS, step_width)
        )
        return carry

    def backward(j, carry):
        rows = group_columns(j)
        frozen = lax.dot_general(
            g_ref[...].reshape(tokens, WIDTH), w_ref[pl.ds(2 * j, 2)].reshape(GROUP, WIDTH),
            contract_last, preferred_element_type=F32,
        )
        adapter = jnp.dot(low_back, down_ref[:, rows], preferred_element_type=F32)
        back_ref[:, :, rows] = (
            (frozen + ADAPTER_SCALE * adapter).astype(BF).reshape(2, COLS, GROUP)
        )
        return carry

    arrived(w_ref.at[:, 1 - core], ws_in.at[0])
    lax.fori_loop(0, 1, backward, 0)
    down_to_sibling.wait_recv()
    acc_ref[1] = (down_part_ref[half_rows(core), :] + down_got_ref[...]).reshape(4, 8, GROUP)
    start_sum(1)

    arrived(att_ref, o_in.at[0])
    low = lax.dot_general(
        att_ref[...].reshape(tokens, WIDTH), down_ref[...], contract_last, preferred_element_type=F32
    ).astype(BF)
    part_ref[...] = (
        factor
        * lax.dot_general(
            low, g_ref[...].reshape(tokens, WIDTH), contract_first, preferred_element_type=F32
        )
    ).astype(BF)

    def phase_a(step):
        tx, tc, target = ring_device(step)
        return remote(
            part_ref.at[half_rows(tc), group_columns(tx)], ra_ref.at[step - 1],
            p_sem.at[2], p_sem.at[3], target,
        )

    for step in range(1, 8):
        phase_a(step).start()

    blocks = WIDTH // step_width
    lax.fori_loop(0, blocks // 2, forward, 0)
    @pl.when(here)
    def _():
        arrived(ks_ref.at[:, :, pl.ds(0, 3)], out_sem.at[0])
        arrived(qs_ref.at[:, pl.ds(0, 3)], out_sem.at[1])
        arrived(ks_ref.at[0, 0, pl.ds(0, 3)], out_sem.at[2])

    @pl.when(jnp.logical_not(here))
    def _():
        arrived(ks_ref, out_sem.at[0])
        arrived(qs_ref, out_sem.at[1])
        arrived(back_low_ref, out_sem.at[2])

    for i in range(2):
        arrived(arrays[i][1].at[:, pl.ds(0, 4)], halo_out.at[i])
    arrived(w_ref.at[0, :, :, pl.ds(0, GROUP)], w_out.at[0])
    arrived(w_ref.at[pl.ds(0, 6), :, :, pl.ds(0, GROUP)], w_out.at[1])
    arrived(w_ref.at[:, :, :, pl.ds(0, GROUP)], w_out.at[2])
    arrived(w_ref.at[:, :, :, pl.ds(0, 2 * GROUP)], w_out.at[3])
    down_to_sibling.wait_send()
    total = part_ref[half_rows(core), group_columns(x)].astype(F32)
    arrived(ra_ref, p_sem.at[3])
    for step in range(1, 8):
        total = total + ra_ref[step - 1].astype(F32)
    acc_ref[0] = total.reshape(4, 8, GROUP)
    start_sum(0)
    finish_sum(1)
    lax.fori_loop(blocks // 2, blocks, forward, 0)
    store_mixed = pltpu.make_async_copy(mixed_ref, mixed_hbm, store_sem.at[1])
    store_mixed.start()
    lax.fori_loop(1, 2, backward, 0)
    finish_sum(0)
    start_round(1)
    lax.fori_loop(2, 3, backward, 0)
    start_round(0)
    pass_round(1)
    lax.fori_loop(3, CHIPS, backward, 0)
    store_back = pltpu.make_async_copy(back_ref, back_hbm, store_sem.at[0])
    store_back.start()
    store_grads = [
        pltpu.make_async_copy(fin_ref.at[a], grads_hbm.at[a], store_sem.at[2 + a]) for a in range(2)
    ]
    pass_round(0)
    finish_round(1)
    store_grads[1].start()
    finish_round(0)
    store_grads[0].start()
    arrived(ra_ref, p_sem.at[2])
    store_back.wait()
    store_mixed.wait()
    store_grads[1].wait()
    store_grads[0].wait()


def deliver_kernel(
    mixed_hbm, back_hbm, grads_hbm, mixed_out, back_out, grad_up_out, grad_down_out,
    held_ref, grads_ref, wide_ref, take_sem, put_sem,
):
    takes = [pltpu.make_async_copy(grads_hbm, grads_ref, take_sem.at[0])]
    puts = []
    for f in range(2):
        for n, (src, dst) in enumerate(((mixed_hbm, mixed_out), (back_hbm, back_out))):
            for half in range(2):
                at = 2 + 4 * f + 2 * n + half
                rows = pl.ds(half * HALF, HALF)
                held = held_ref.at[n, f, rows]
                takes.append(pltpu.make_async_copy(src.at[f, rows], held, take_sem.at[at]))
                puts.append(pltpu.make_async_copy(held, dst.at[f, rows], put_sem.at[at]))
    for copy in takes:
        copy.start()
    for n, dst in enumerate((grad_up_out, grad_down_out)):
        if n == 0:
            takes[0].wait()
        wide_ref[n] = grads_ref[n].astype(F32)
        copy = pltpu.make_async_copy(wide_ref.at[n], dst, put_sem.at[n])
        copy.start()
        puts.append(copy)
    for take, put in zip(takes[1:], puts[:8]):
        take.wait()
        put.start()
    for copy in puts:
        copy.wait()


def per_device(
    queries, keys, values, head_window_radius, output_weight, adapter_down_weight, adapter_up_weight,
    output_gradient,
):
    factor = ADAPTER_SCALE / math.sqrt(GRID * GRID * COLS)
    smem = pl.BlockSpec(memory_space=pltpu.SMEM)
    hbm = pl.BlockSpec(memory_space=pl.ANY)
    block = jax.ShapeDtypeStruct((2, COLS, WIDTH), BF)
    dma = pltpu.SemaphoreType.DMA
    small = jax.ShapeDtypeStruct((RANK, WIDTH), F32)
    mixed, back, grads = pl.pallas_call(
        functools.partial(step_kernel, factor),
        out_shape=(block, block, jax.ShapeDtypeStruct((2, RANK, WIDTH), BF)),
        in_specs=[smem, hbm, hbm, hbm, hbm, hbm, hbm, hbm],
        out_specs=(hbm,) * 3,
        scratch_shapes=[
            pltpu.VMEM((2, COLS, WIDTH), BF),
            pltpu.VMEM((2, COLS, WIDTH), BF),
            pltpu.VMEM((GROUP_HEADS, 4, 2, COLS, HEAD_DIM), BF),
            pltpu.VMEM((GROUP_HEADS, 6, 4, COLS, HEAD_DIM), BF),
            pltpu.VMEM((GROUP_HEADS, 6, 4, COLS, HEAD_DIM), BF),
            pltpu.VMEM((GROUP_HEADS, 4, 2, COLS, HEAD_DIM), BF),
            pltpu.VMEM((8, 2, COLS, WIDTH), BF),
            pltpu.VMEM((2, COLS, WIDTH), BF),
            pltpu.VMEM((2, COLS, WIDTH), BF),
            pltpu.VMEM((RANK, WIDTH), BF),
            pltpu.VMEM((7, 32, GROUP), BF),
            pltpu.VMEM((2, 4, 8, GROUP), F32),
            pltpu.VMEM((2, 16, 8, GROUP), F32),
            pltpu.VMEM((2, 4, 8, GROUP), F32),
            pltpu.VMEM((2, 32, GROUP), BF),
            pltpu.VMEM((2, RANK, WIDTH), BF),
            pltpu.VMEM((RANK, WIDTH), BF),
            pltpu.VMEM((RANK, WIDTH), BF),
            pltpu.VMEM((COLS, 2 * RANK), BF),
            pltpu.VMEM((2, 2, COLS, 2 * RANK), BF),
            pltpu.VMEM((4, 2, RANK, COLS), BF),
            pltpu.VMEM((RANK, GROUP), F32),
            pltpu.VMEM((32, GROUP), F32),
            dma((5,)), dma((3,)), dma((3, GROUP_HEADS)), dma((2,)), dma((2, GROUP_HEADS, 2)),
            dma((2,)), dma((4,)),
            dma((4,)), dma((2,)), dma((2, 3)), dma((2, 4)), dma((1,)), dma((2, 6)), dma((2, 4)), dma((4,)),
        ],
        compiler_params=pltpu.CompilerParams(
            collective_id=0, has_side_effects=True, vmem_limit_bytes=57 * 2**20
        ),
        cost_estimate=pl.CostEstimate(
            flops=14_000_000_000, bytes_accessed=100_000_000, transcendentals=7_000_000
        ),
        name="training_step",
    )(
        head_window_radius.T, queries, keys, values, output_weight,
        output_gradient.reshape(2, COLS, WIDTH), adapter_down_weight.T, adapter_up_weight,
    )
    mixed, back, grad_up, grad_down = pl.pallas_call(
        deliver_kernel,
        out_shape=(block, block, small, small),
        in_specs=[hbm] * 3,
        out_specs=(hbm,) * 4,
        scratch_shapes=[
            pltpu.VMEM((2, 2, COLS, WIDTH), BF),
            pltpu.VMEM((2, RANK, WIDTH), BF),
            pltpu.VMEM((2, RANK, WIDTH), F32),
            dma((10,)),
            dma((10,)),
        ],
        compiler_params=pltpu.CompilerParams(vmem_limit_bytes=60 * 2**20),
        name="deliver",
    )(mixed, back, grads)
    shape = (2, 1, COLS, WIDTH)
    return mixed.reshape(shape), back.reshape(shape), grad_up, grad_down.T


def solution(mesh):
    tokens = P("tm", "height", None, None)
    return jax.shard_map(
        per_device,
        mesh=mesh,
        in_specs=(tokens, tokens, tokens, P(), P("height", None), P(), P(), tokens),
        out_specs=(tokens, tokens, P(), P()),
        check_vma=False,
    )
```

```python
import functools
import math

import jax
import jax.numpy as jnp
from jax import lax
from jax.experimental import pallas as pl
from jax.experimental.pallas import tpu as pltpu
from jax.sharding import PartitionSpec as P

HEADS = 20
HEAD_DIM = 128
TILE_W = 16
COLS = 160
HALF = COLS // 2
WINDOW = 128
RANK = 64
ADAPTER_SCALE = 2.0
GRID = 16
CHIPS = 4
GROUP_HEADS = HEADS // CHIPS
GROUP = GROUP_HEADS * HEAD_DIM
WIDTH = HEADS * HEAD_DIM
NEG = -1e30
MESH = pl.DeviceIdType.MESH
BF = jnp.bfloat16
F32 = jnp.float32


def place():
    tm, height = lax.axis_index("tm"), lax.axis_index("height")
    z, xh = tm // 2, tm % 2
    y, xl, core = height // 4, (height // 2) % 2, height % 2
    return z, xh, y, xl, core


def device(z, x, y, core):
    return (z * 2 + x // 2, y * 4 + (x % 2) * 2 + core)


def enter(partners):
    barrier = pltpu.get_barrier_semaphore()
    for partner in partners:
        pl.semaphore_signal(barrier, inc=1, device_id=partner, device_id_type=MESH)
    pl.semaphore_wait(barrier, len(partners))


def remote(src, dst, send, recv, target):
    return pltpu.make_async_remote_copy(
        src_ref=src, dst_ref=dst, send_sem=send, recv_sem=recv, device_id=target, device_id_type=MESH
    )


def arrived(dst, sem):
    pltpu.make_async_copy(dst, dst, sem).wait()


def group_columns(x):
    return pl.ds(pl.multiple_of(x * GROUP, 128), GROUP)


def attend(j, f, half, radii, frame, row_first, q_ref, k_ref, v_ref, o_ref):
    radius_frame, radius_row, radius_column = radii
    start = (COLS - WINDOW) * half
    query_tile = (lax.broadcasted_iota(jnp.int32, (HALF, WINDOW), 0) + half * HALF) // TILE_W
    key_tile = (lax.broadcasted_iota(jnp.int32, (HALF, WINDOW), 1) + start) // TILE_W
    near = jnp.abs(query_tile - key_tile) <= radius_column
    query_rows, key_rows = pl.ds(half * HALF, HALF), pl.ds(start, WINDOW)
    places = [(a, b) for a in range(3) for b in range(4)]
    q = jnp.concatenate([q_ref[j, f, r, query_rows, :] for r in range(2)], axis=0)
    k = jnp.concatenate([k_ref[j, f + a, b, key_rows, :] for a, b in places], axis=0)
    v = jnp.concatenate([v_ref[j, f + a, b, key_rows, :] for a, b in places], axis=0)
    scores = lax.dot_general(q, k, (((1,), (1,)), ((), ())), preferred_element_type=F32)
    scale = math.log2(math.e) / math.sqrt(HEAD_DIM)
    nothing = jnp.zeros((HALF, WINDOW), BF)
    rows = []
    for r in range(2):
        masked = {}
        for at, (a, b) in enumerate(places):
            if not r <= b <= r + 2:
                continue
            s = scores[r * HALF : (r + 1) * HALF, at * WINDOW : (at + 1) * WINDOW]
            allowed = near
            if a != 1 or b != r + 1:
                other_frame, other_row = frame + (a - 1), row_first + (b - 1)
                inside = (
                    (other_frame >= 0) & (other_frame < GRID) & (other_row >= 0) & (other_row < GRID)
                )
                if a != 1:
                    inside = inside & (radius_frame > 0)
                if b != r + 1:
                    inside = inside & (radius_row > 0)
                allowed = near & inside
            masked[a, b] = jnp.where(allowed, s, NEG)
        highest = jnp.max(functools.reduce(jnp.maximum, masked.values()), axis=1, keepdims=True)
        weights = {at: jnp.exp2((s - highest) * scale) for at, s in masked.items()}
        total = jnp.sum(functools.reduce(jnp.add, weights.values()), axis=1, keepdims=True)
        share = 1.0 / total
        rows.append(
            jnp.concatenate(
                [(weights[at] * share).astype(BF) if at in weights else nothing for at in places], axis=1
            )
        )
    result = jnp.dot(jnp.concatenate(rows, axis=0), v, preferred_element_type=F32).astype(BF)
    for r in range(2):
        o_ref[j, f, r, query_rows, :] = result[r * HALF : (r + 1) * HALF]


def step_kernel(
    factor, radius_ref, q_hbm, k_hbm, v_hbm, w_hbm, g_hbm, down_hbm, up_hbm,
    mixed_hbm, back_hbm, grads_hbm,
    mixed_ref, back_ref,
    qs_ref, ks_ref, vs_ref, os_ref, w_ref, g_ref, att_ref,
    part_ref, ra_ref, acc_ref, rb_ref, rd_ref, rounded_ref, fin_ref,
    down_ref, up_ref, own_back_ref, back_low_ref, back_turned_ref, down_part_ref, down_got_ref,
    load_sem, out_sem, in_sem, halo_out, halo_in, o_in, p_sem,
    w_out, wx_in, wy_in, wz_in, ws_in, r_sem, e_in, store_sem,
):
    z, xh, y, xl, core = place()
    x = xh * 2 + xl
    here = xl == core
    ring = x * 2 + core
    band = y * 2 + core
    before, after = (band + 7) % 8, (band + 1) % 8
    left = device(z, x, before // 2, before % 2)
    right = device(z, x, after // 2, after % 2)
    sibling = device(z, x, y, 1 - core)

    def ring_device(step):
        other = (ring + step) % 8
        return other // 2, other % 2, device(z, other // 2, y, other % 2)

    def y_device(step):
        return device(z, x, (y + step) % 4, core)

    def z_device(step):
        return device((z + step) % 4, x, y, core)

    up, down = z_device(3), z_device(1)

    def head_columns(chip, j):
        return pl.ds(pl.multiple_of((chip * GROUP_HEADS + j) * HEAD_DIM, HEAD_DIM), HEAD_DIM)

    load_gradient = pltpu.make_async_copy(g_hbm, g_ref, load_sem.at[0])
    load_weight = [
        pltpu.make_async_copy(
            w_hbm.at[:, group_columns((z + quarter) % 4)],
            w_ref.at[y * 2 + xl, core, :, group_columns((z + quarter) % 4)],
            load_sem.at[1 + quarter // 2],
        )
        for quarter in (0, 2)
    ]
    load_up = pltpu.make_async_copy(up_hbm, up_ref, load_sem.at[3])
    load_down = pltpu.make_async_copy(down_hbm, down_ref, load_sem.at[4])
    load_gradient.start()
    load_up.start()
    load_down.start()
    for copy in load_weight:
        copy.start()

    outside = (band + 7 + 2 * core) % 8
    enter(
        [ring_device(step)[2] for step in range(1, 8)]
        + [device((z + step % 4) % 4, x, (y + step // 4) % 4, core) for step in range(1, 16)]
        + [device(z, x, outside // 2, outside % 2)]
    )

    arrays = ((k_hbm, ks_ref, 1), (v_hbm, vs_ref, 1), (q_hbm, qs_ref, 0))

    def exchange(i, j, step):
        src, dst, pad = arrays[i]
        target = (x + step) % CHIPS
        piece = src.at[:, 0, :, head_columns(target, j)]
        slot = dst.at[j, pl.ds(pad + 2 * xh, 2), pad + core]
        return piece, slot, remote(
            piece, slot, out_sem.at[0], in_sem.at[i, j],
            device(z, target, y, xl),
        )

    def give(i, j):
        for step in (2, 1, 3):
            exchange(i, j, step)[2].start()
        piece, slot, copy = exchange(i, j, 0)

        @pl.when(here)
        def _():
            pltpu.make_async_copy(piece, slot, in_sem.at[i, j]).start()

        @pl.when(jnp.logical_not(here))
        def _():
            copy.start()

    def landed(i, j):
        own = (pl.ds(1, 4), pl.ds(1, 2)) if i < 2 else ()
        arrived(arrays[i][1].at[(j, *own)], in_sem.at[i, j])

    def halos(i, j):
        ref = arrays[i][1].at[j]

        def send(n, src, dst, target):
            return remote(src, dst, halo_out.at[i], halo_in.at[i, j, min(n // 2, 1)], target)

        rows, own = pl.ds(1, 2), pl.ds(1, 4)
        return (
            send(0, ref.at[1, rows], ref.at[5, rows], up),
            send(1, ref.at[4, rows], ref.at[0, rows], down),
            send(2, ref.at[own, 1], ref.at[own, 3], left),
            send(3, ref.at[own, 2], ref.at[own, 0], right),
            send(4, ref.at[0, 1], ref.at[0, 3], left),
            send(5, ref.at[5, 1], ref.at[5, 3], left),
            send(6, ref.at[0, 2], ref.at[0, 0], right),
            send(7, ref.at[5, 2], ref.at[5, 0], right),
        )

    def start_halos(j):
        for i in range(2):
            landed(i, j)
            for copy in halos(i, j)[:4]:
                copy.start()

    def start_corners(j):
        for i in range(2):
            arrived(arrays[i][1].at[j, 0], halo_in.at[i, j, 0])
            for copy in halos(i, j)[4:]:
                copy.start()

    def await_head(j):
        for i in range(2):
            arrived(arrays[i][1].at[j, pl.ds(0, 3)], halo_in.at[i, j, 1])
        landed(2, j)

    def attend_frames(j, first, last, midway=None):
        head = x * GROUP_HEADS + j
        radii = [radius_ref[n, head] for n in range(3)]

        def one(f, carry):
            if midway is not None:
                pl.when(f == 2)(midway)
            for half in range(2):
                attend(
                    j, f, half, radii, z * 4 + f, y * 4 + core * 2, qs_ref, ks_ref, vs_ref, os_ref
                )
            return carry

        lax.fori_loop(first, last, one, 0)

    def give_back(j, n):
        frames = (xh + n // 2) % 2
        row = (core + n % 2) % 2
        piece = os_ref.at[j, pl.ds(2 * frames, 2), row]
        slot = att_ref.at[:, :, head_columns(x, j)]
        return piece, slot, remote(
            piece, slot, out_sem.at[1], o_in.at[0], device(z, frames * 2 + core, y, row)
        )

    def start_back(j, near=True, far=True):
        if far:
            give_back(j, 2)[2].start()
            give_back(j, 3)[2].start()
        if not near:
            return
        give_back(j, 1)[2].start()
        piece, slot, copy = give_back(j, 0)

        @pl.when(here)
        def _():
            pltpu.make_async_copy(piece, slot, o_in.at[0]).start()

        @pl.when(jnp.logical_not(here))
        def _():
            copy.start()

    def weight_piece(quarter, n, side):
        return w_ref.at[pl.ds(2 * ((y + n) % 4), 2), side, :, group_columns((z + quarter) % 4)]

    def weight_shard(quarter, n, part):
        return w_ref.at[
            2 * ((y + n) % 4) + (xl + part) % 2, core, :, group_columns((z + quarter) % 4)
        ]

    weight_x = remote(
        weight_shard(0, 0, 0), weight_shard(0, 0, 0), w_out.at[0], wx_in.at[0],
        device(z, (xh + core) % 2 * 2 + 1 - xl, y, core),
    )
    weight_across = remote(
        weight_shard(0, 0, 1), weight_shard(0, 0, 1), w_out.at[0], wx_in.at[1], z_device(2)
    )

    def weight_y(quarter, step, part):
        piece = weight_shard(quarter, 0, part)
        at = quarter // 2
        return remote(
            piece, piece, w_out.at[1], wy_in.at[at, 3 - step],
            y_device(step),
        )

    def weight_z(way, n, part):
        piece = weight_shard(0, n, part)
        return remote(piece, piece, w_out.at[2], wz_in.at[way, n], (up, down)[way])

    def weight_sibling(quarter, n):
        piece = weight_piece(quarter, n, core)
        return remote(piece, piece, w_out.at[3], ws_in.at[0], sibling)

    def start_y(quarter, part, steps=(1, 3, 2)):
        for step in steps:
            weight_y(quarter, step, part).start()

    def start_z(n, part):
        for way in range(2):
            weight_z(way, n, part).start()

    def take_y(quarter, n):
        arrived(weight_piece(quarter, n, core), wy_in.at[quarter // 2, n - 1])
        weight_sibling(quarter, n).start()

    def take_z(n):
        for way, quarter in ((0, 1), (1, 3)):
            arrived(weight_piece(quarter, n, core), wz_in.at[way, n])
            weight_sibling(quarter, n).start()

    def give_low(step):
        target = (x + step) % CHIPS
        return remote(
            own_back_ref, back_low_ref.at[xh, core], out_sem.at[2], o_in.at[1],
            device(z, target, y, xl),
        )

    def add_down(j):
        total = jnp.zeros((RANK, HEAD_DIM), F32)
        for f in range(4):
            for r in range(2):
                total = total + jnp.dot(
                    back_turned_ref[f, r], os_ref[j, f, r], preferred_element_type=F32
                )
        down_part_ref[:, j * HEAD_DIM : (j + 1) * HEAD_DIM] = factor * total

    def half_rows(n):
        return pl.ds(pl.multiple_of(n * 32, 32), 32)

    down_to_sibling = remote(
        down_part_ref.at[half_rows(1 - core)], down_got_ref, p_sem.at[0], p_sem.at[1], sibling
    )

    def start_sum(a):
        for step in range(1, 16):
            sum_copy(a, step).start()
        rb_ref[a, y * 4 + z] = acc_ref[a, y]

    def sum_copy(a, step):
        dy, dz = step // 4, step % 4
        return remote(
            acc_ref.at[a, (y + dy) % 4], rb_ref.at[a, y * 4 + z], r_sem.at[a, 0], r_sem.at[a, 1],
            device((z + dz) % 4, x, (y + dy) % 4, core),
        )

    def round_y(a, step):
        return remote(
            rd_ref.at[a, y], rd_ref.at[a, y], r_sem.at[a, 2], r_sem.at[a, 3], y_device(step)
        )

    def finish_sum(a):
        arrived(rb_ref.at[a, pl.ds(0, 15)], r_sem.at[a, 1])
        total = rb_ref[a, 0]
        for source in range(1, 16):
            total = total + rb_ref[a, source]
        rd_ref[a, y] = total
        for step in range(1, 4):
            round_y(a, step).start()

    def share(a, tx, tc):
        return fin_ref.at[a, half_rows(tc), group_columns(tx)]

    def round_x(a, step):
        return remote(
            rounded_ref.at[a], share(a, x, core), r_sem.at[a, 4], e_in.at[a, step],
            device(z, (x + step) % CHIPS, y, core),
        )

    def pass_share(a, step):
        piece = share(a, (x + CHIPS - step) % CHIPS, core)
        return remote(piece, piece, r_sem.at[a, 5], e_in.at[a, 0], sibling)

    def start_round(a):
        arrived(rb_ref.at[a, pl.ds(0, 3)], r_sem.at[a, 3])
        rounded_ref[a] = rd_ref[a].reshape(32, GROUP).astype(BF)
        for step in (2, 1, 3):
            round_x(a, step).start()
        fin_ref[a, half_rows(core), group_columns(x)] = rounded_ref[a]
        pass_share(a, 0).start()

    def pass_round(a):
        for step in (1, 3, 2):
            arrived(share(a, (x + CHIPS - step) % CHIPS, core), e_in.at[a, step])
            pass_share(a, step).start()

    def finish_round(a):
        arrived(fin_ref.at[a, half_rows(1 - core)], e_in.at[a, 0])
        arrived(rb_ref.at[a, pl.ds(0, 15)], r_sem.at[a, 0])
        arrived(rb_ref.at[a, pl.ds(0, 3)], r_sem.at[a, 2])
        arrived(fin_ref.at[a, pl.ds(0, 32), pl.ds(0, 3 * GROUP)], r_sem.at[a, 4])
        arrived(fin_ref.at[a, pl.ds(0, 32)], r_sem.at[a, 5])

    K, V, Q = 0, 1, 2
    for copy in load_weight:
        copy.wait()
    weight_x.start()
    start_y(0, 0)
    start_z(0, 0)
    give(K, 0)
    give(V, 0)
    load_gradient.wait()
    load_up.wait()
    load_down.wait()
    contract_last = (((1,), (1,)), ((), ()))
    contract_first = (((0,), (0,)), ((), ()))
    tokens = 2 * COLS
    low_back = lax.dot_general(
        g_ref[...].reshape(tokens, WIDTH), up_ref[...], contract_last, preferred_element_type=F32
    ).astype(BF)
    own_back_ref[...] = jnp.concatenate([low_back[:COLS], low_back[COLS:]], axis=1)
    for step in (2, 1, 3):
        give_low(step).start()
    low_copy = give_low(0)
    low_slot = back_low_ref.at[xh, core]

    @pl.when(here)
    def _():
        pltpu.make_async_copy(own_back_ref, low_slot, o_in.at[1]).start()

    @pl.when(jnp.logical_not(here))
    def _():
        low_copy.start()

    for i, j in (
        (K, 1), (V, 1), (Q, 0), (K, 2), (V, 2), (Q, 1),
        (K, 3), (V, 3), (Q, 2), (K, 4), (V, 4), (Q, 3), (Q, 4),
    ):
        give(i, j)
    weight_x.wait_recv()
    start_y(0, 1)
    start_z(0, 1)
    weight_sibling(0, 0).start()

    start_halos(0)
    start_corners(0)
    take_y(0, 1)
    start_z(1, 0)
    start_halos(1)
    arrived(back_low_ref, o_in.at[1])
    for pair in range(2):
        for row in range(2):
            turned = back_low_ref[pair, row].astype(F32).T.astype(BF)
            for n in range(2):
                frame = 2 * pair + n
                back_turned_ref[frame, row] = turned[n * RANK : (n + 1) * RANK]
    await_head(0)
    start_z(1, 1)
    start_y(2, 0, (1, 3))
    attend_frames(0, 0, 4, functools.partial(start_corners, 1))
    start_back(0)
    add_down(0)

    start_halos(2)
    await_head(1)
    start_y(2, 0, (2,))
    weight_across.start()
    take_z(0)
    attend_frames(1, 0, 4, functools.partial(start_corners, 2))
    start_back(1)
    add_down(1)

    start_halos(3)
    await_head(2)
    arrived(weight_shard(2, 0, 1), wx_in.at[1])
    weight_sibling(2, 0).start()
    start_y(2, 1, (1, 3))
    take_y(0, 3)
    start_z(3, 0)
    take_z(1)
    attend_frames(2, 0, 4, functools.partial(start_corners, 3))
    start_back(2)
    add_down(2)

    start_halos(4)
    await_head(3)
    start_y(2, 1, (2,))
    start_z(3, 1)
    take_y(0, 2)
    start_z(2, 0)
    start_z(2, 1)
    attend_frames(3, 0, 4, functools.partial(start_corners, 4))
    start_back(3)
    add_down(3)
    for n in range(1, 4):
        take_y(2, n)
    await_head(4)
    far_frames = 2 * (1 - xh)
    attend_frames(4, far_frames, far_frames + 2)
    start_back(4, near=False)
    attend_frames(4, 2 - far_frames, 4 - far_frames)
    start_back(4, far=False)
    add_down(4)
    down_to_sibling.start()
    take_z(3)
    take_z(2)

    step_width = 256

    def forward(j, carry):
        columns = pl.ds(pl.multiple_of(j * step_width, step_width), step_width)
        frozen = jnp.dot(
            att_ref[...].reshape(tokens, WIDTH), w_ref[:, :, :, columns].reshape(WIDTH, step_width),
            preferred_element_type=F32,
        )
        adapter = jnp.dot(low, up_ref[:, columns], preferred_element_type=F32)
        mixed_ref[:, :, columns] = (
            (frozen + ADAPTER_SCALE * adapter).astype(BF).reshape(2, COLS, step_width)
        )
        return carry

    def backward(j, carry):
        rows = group_columns(j)
        frozen = lax.dot_general(
            g_ref[...].reshape(tokens, WIDTH), w_ref[pl.ds(2 * j, 2)].reshape(GROUP, WIDTH),
            contract_last, preferred_element_type=F32,
        )
        adapter = jnp.dot(low_back, down_ref[:, rows], preferred_element_type=F32)
        back_ref[:, :, rows] = (
            (frozen + ADAPTER_SCALE * adapter).astype(BF).reshape(2, COLS, GROUP)
        )
        return carry

    down_to_sibling.wait_recv()
    acc_ref[1] = (down_part_ref[half_rows(core), :] + down_got_ref[...]).reshape(4, 8, GROUP)
    start_sum(1)

    arrived(att_ref, o_in.at[0])
    low = lax.dot_general(
        att_ref[...].reshape(tokens, WIDTH), down_ref[...], contract_last, preferred_element_type=F32
    ).astype(BF)
    part_ref[...] = (
        factor
        * lax.dot_general(
            low, g_ref[...].reshape(tokens, WIDTH), contract_first, preferred_element_type=F32
        )
    ).astype(BF)

    def phase_a(step):
        tx, tc, target = ring_device(step)
        return remote(
            part_ref.at[half_rows(tc), group_columns(tx)], ra_ref.at[step - 1],
            p_sem.at[2], p_sem.at[3], target,
        )

    for step in range(1, 8):
        phase_a(step).start()

    blocks = WIDTH // step_width
    arrived(w_ref.at[:, 1 - core], ws_in.at[0])
    lax.fori_loop(0, blocks // 2, forward, 0)
    @pl.when(here)
    def _():
        arrived(ks_ref.at[:, :, pl.ds(0, 3)], out_sem.at[0])
        arrived(qs_ref.at[:, pl.ds(0, 3)], out_sem.at[1])
        arrived(ks_ref.at[0, 0, pl.ds(0, 3)], out_sem.at[2])

    @pl.when(jnp.logical_not(here))
    def _():
        arrived(ks_ref, out_sem.at[0])
        arrived(qs_ref, out_sem.at[1])
        arrived(back_low_ref, out_sem.at[2])

    for i in range(2):
        arrived(arrays[i][1].at[:, pl.ds(0, 4)], halo_out.at[i])
    arrived(w_ref.at[0, :, :, pl.ds(0, GROUP)], w_out.at[0])
    arrived(w_ref.at[pl.ds(0, 6), :, :, pl.ds(0, GROUP)], w_out.at[1])
    arrived(w_ref.at[:, :, :, pl.ds(0, GROUP)], w_out.at[2])
    arrived(w_ref.at[:, :, :, pl.ds(0, 2 * GROUP)], w_out.at[3])
    down_to_sibling.wait_send()
    total = part_ref[half_rows(core), group_columns(x)].astype(F32)
    arrived(ra_ref, p_sem.at[3])
    for step in range(1, 8):
        total = total + ra_ref[step - 1].astype(F32)
    acc_ref[0] = total.reshape(4, 8, GROUP)
    start_sum(0)
    finish_sum(1)
    lax.fori_loop(blocks // 2, blocks, forward, 0)
    store_mixed = pltpu.make_async_copy(mixed_ref, mixed_hbm, store_sem.at[1])
    store_mixed.start()
    lax.fori_loop(0, 2, backward, 0)
    finish_sum(0)
    start_round(1)
    lax.fori_loop(2, 3, backward, 0)
    start_round(0)
    pass_round(1)
    lax.fori_loop(3, CHIPS, backward, 0)
    store_back = pltpu.make_async_copy(back_ref, back_hbm, store_sem.at[0])
    store_back.start()
    store_grads = [
        pltpu.make_async_copy(fin_ref.at[a], grads_hbm.at[a], store_sem.at[2 + a]) for a in range(2)
    ]
    pass_round(0)
    finish_round(1)
    store_grads[1].start()
    finish_round(0)
    store_grads[0].start()
    arrived(ra_ref, p_sem.at[2])
    store_back.wait()
    store_mixed.wait()
    store_grads[1].wait()
    store_grads[0].wait()


def deliver_kernel(
    mixed_hbm, back_hbm, grads_hbm, mixed_out, back_out, grad_up_out, grad_down_out,
    held_ref, grads_ref, wide_ref, take_sem, put_sem,
):
    takes = [pltpu.make_async_copy(grads_hbm, grads_ref, take_sem.at[0])]
    puts = []
    for f in range(2):
        for n, (src, dst) in enumerate(((mixed_hbm, mixed_out), (back_hbm, back_out))):
            for half in range(2):
                at = 2 + 4 * f + 2 * n + half
                rows = pl.ds(half * HALF, HALF)
                held = held_ref.at[n, f, rows]
                takes.append(pltpu.make_async_copy(src.at[f, rows], held, take_sem.at[at]))
                puts.append(pltpu.make_async_copy(held, dst.at[f, rows], put_sem.at[at]))
    for copy in takes:
        copy.start()
    for n, dst in enumerate((grad_up_out, grad_down_out)):
        if n == 0:
            takes[0].wait()
        wide_ref[n] = grads_ref[n].astype(F32)
        copy = pltpu.make_async_copy(wide_ref.at[n], dst, put_sem.at[n])
        copy.start()
        puts.append(copy)
    for take, put in zip(takes[1:], puts[:8]):
        take.wait()
        put.start()
    for copy in puts:
        copy.wait()


def per_device(
    queries, keys, values, head_window_radius, output_weight, adapter_down_weight, adapter_up_weight,
    output_gradient,
):
    factor = ADAPTER_SCALE / math.sqrt(GRID * GRID * COLS)
    smem = pl.BlockSpec(memory_space=pltpu.SMEM)
    hbm = pl.BlockSpec(memory_space=pl.ANY)
    block = jax.ShapeDtypeStruct((2, COLS, WIDTH), BF)
    dma = pltpu.SemaphoreType.DMA
    small = jax.ShapeDtypeStruct((RANK, WIDTH), F32)
    mixed, back, grads = pl.pallas_call(
        functools.partial(step_kernel, factor),
        out_shape=(block, block, jax.ShapeDtypeStruct((2, RANK, WIDTH), BF)),
        in_specs=[smem, hbm, hbm, hbm, hbm, hbm, hbm, hbm],
        out_specs=(hbm,) * 3,
        scratch_shapes=[
            pltpu.VMEM((2, COLS, WIDTH), BF),
            pltpu.VMEM((2, COLS, WIDTH), BF),
            pltpu.VMEM((GROUP_HEADS, 4, 2, COLS, HEAD_DIM), BF),
            pltpu.VMEM((GROUP_HEADS, 6, 4, COLS, HEAD_DIM), BF),
            pltpu.VMEM((GROUP_HEADS, 6, 4, COLS, HEAD_DIM), BF),
            pltpu.VMEM((GROUP_HEADS, 4, 2, COLS, HEAD_DIM), BF),
            pltpu.VMEM((8, 2, COLS, WIDTH), BF),
            pltpu.VMEM((2, COLS, WIDTH), BF),
            pltpu.VMEM((2, COLS, WIDTH), BF),
            pltpu.VMEM((RANK, WIDTH), BF),
            pltpu.VMEM((7, 32, GROUP), BF),
            pltpu.VMEM((2, 4, 8, GROUP), F32),
            pltpu.VMEM((2, 16, 8, GROUP), F32),
            pltpu.VMEM((2, 4, 8, GROUP), F32),
            pltpu.VMEM((2, 32, GROUP), BF),
            pltpu.VMEM((2, RANK, WIDTH), BF),
            pltpu.VMEM((RANK, WIDTH), BF),
            pltpu.VMEM((RANK, WIDTH), BF),
            pltpu.VMEM((COLS, 2 * RANK), BF),
            pltpu.VMEM((2, 2, COLS, 2 * RANK), BF),
            pltpu.VMEM((4, 2, RANK, COLS), BF),
            pltpu.VMEM((RANK, GROUP), F32),
            pltpu.VMEM((32, GROUP), F32),
            dma((5,)), dma((3,)), dma((3, GROUP_HEADS)), dma((2,)), dma((2, GROUP_HEADS, 2)),
            dma((2,)), dma((4,)),
            dma((4,)), dma((2,)), dma((2, 3)), dma((2, 4)), dma((1,)), dma((2, 6)), dma((2, 4)), dma((4,)),
        ],
        compiler_params=pltpu.CompilerParams(
            collective_id=0, has_side_effects=True, vmem_limit_bytes=57 * 2**20
        ),
        cost_estimate=pl.CostEstimate(
            flops=14_000_000_000, bytes_accessed=100_000_000, transcendentals=7_000_000
        ),
        name="training_step",
    )(
        head_window_radius.T, queries, keys, values, output_weight,
        output_gradient.reshape(2, COLS, WIDTH), adapter_down_weight.T, adapter_up_weight,
    )
    mixed, back, grad_up, grad_down = pl.pallas_call(
        deliver_kernel,
        out_shape=(block, block, small, small),
        in_specs=[hbm] * 3,
        out_specs=(hbm,) * 4,
        scratch_shapes=[
            pltpu.VMEM((2, 2, COLS, WIDTH), BF),
            pltpu.VMEM((2, RANK, WIDTH), BF),
            pltpu.VMEM((2, RANK, WIDTH), F32),
            dma((10,)),
            dma((10,)),
        ],
        compiler_params=pltpu.CompilerParams(vmem_limit_bytes=60 * 2**20),
        name="deliver",
    )(mixed, back, grads)
    shape = (2, 1, COLS, WIDTH)
    return mixed.reshape(shape), back.reshape(shape), grad_up, grad_down.T


def solution(mesh):
    tokens = P("tm", "height", None, None)
    return jax.shard_map(
        per_device,
        mesh=mesh,
        in_specs=(tokens, tokens, tokens, P(), P("height", None), P(), P(), tokens),
        out_specs=(tokens, tokens, P(), P()),
        check_vma=False,
    )
```

```python
import functools
import math

import jax
import jax.numpy as jnp
from jax import lax
from jax.experimental import pallas as pl
from jax.experimental.pallas import tpu as pltpu
from jax.sharding import PartitionSpec as P

HEADS = 20
HEAD_DIM = 128
TILE_W = 16
COLS = 160
HALF = COLS // 2
WINDOW = 128
RANK = 64
ADAPTER_SCALE = 2.0
GRID = 16
CHIPS = 4
GROUP_HEADS = HEADS // CHIPS
GROUP = GROUP_HEADS * HEAD_DIM
WIDTH = HEADS * HEAD_DIM
NEG = -1e30
MESH = pl.DeviceIdType.MESH
BF = jnp.bfloat16
F32 = jnp.float32


def place():
    tm, height = lax.axis_index("tm"), lax.axis_index("height")
    z, xh = tm // 2, tm % 2
    y, xl, core = height // 4, (height // 2) % 2, height % 2
    return z, xh, y, xl, core


def device(z, x, y, core):
    return (z * 2 + x // 2, y * 4 + (x % 2) * 2 + core)


def enter(partners):
    barrier = pltpu.get_barrier_semaphore()
    for partner in partners:
        pl.semaphore_signal(barrier, inc=1, device_id=partner, device_id_type=MESH)
    pl.semaphore_wait(barrier, len(partners))


def remote(src, dst, send, recv, target):
    return pltpu.make_async_remote_copy(
        src_ref=src, dst_ref=dst, send_sem=send, recv_sem=recv, device_id=target, device_id_type=MESH
    )


def arrived(dst, sem):
    pltpu.make_async_copy(dst, dst, sem).wait()


def group_columns(x):
    return pl.ds(pl.multiple_of(x * GROUP, 128), GROUP)


def attend(j, f, half, radii, frame, row_first, q_ref, k_ref, v_ref, o_ref):
    radius_frame, radius_row, radius_column = radii
    start = (COLS - WINDOW) * half
    query_tile = (lax.broadcasted_iota(jnp.int32, (HALF, WINDOW), 0) + half * HALF) // TILE_W
    key_tile = (lax.broadcasted_iota(jnp.int32, (HALF, WINDOW), 1) + start) // TILE_W
    near = jnp.abs(query_tile - key_tile) <= radius_column
    query_rows, key_rows = pl.ds(half * HALF, HALF), pl.ds(start, WINDOW)
    places = [(a, b) for a in range(3) for b in range(4)]
    q = jnp.concatenate([q_ref[j, f, r, query_rows, :] for r in range(2)], axis=0)
    k = jnp.concatenate([k_ref[j, f + a, b, key_rows, :] for a, b in places], axis=0)
    v = jnp.concatenate([v_ref[j, f + a, b, key_rows, :] for a, b in places], axis=0)
    scores = lax.dot_general(q, k, (((1,), (1,)), ((), ())), preferred_element_type=F32)
    scale = math.log2(math.e) / math.sqrt(HEAD_DIM)
    nothing = jnp.zeros((HALF, WINDOW), BF)
    rows = []
    for r in range(2):
        masked = {}
        for at, (a, b) in enumerate(places):
            if not r <= b <= r + 2:
                continue
            s = scores[r * HALF : (r + 1) * HALF, at * WINDOW : (at + 1) * WINDOW]
            allowed = near
            if a != 1 or b != r + 1:
                other_frame, other_row = frame + (a - 1), row_first + (b - 1)
                inside = (
                    (other_frame >= 0) & (other_frame < GRID) & (other_row >= 0) & (other_row < GRID)
                )
                if a != 1:
                    inside = inside & (radius_frame > 0)
                if b != r + 1:
                    inside = inside & (radius_row > 0)
                allowed = near & inside
            masked[a, b] = jnp.where(allowed, s, NEG)
        highest = jnp.max(functools.reduce(jnp.maximum, masked.values()), axis=1, keepdims=True)
        weights = {at: jnp.exp2((s - highest) * scale) for at, s in masked.items()}
        total = jnp.sum(functools.reduce(jnp.add, weights.values()), axis=1, keepdims=True)
        share = 1.0 / total
        rows.append(
            jnp.concatenate(
                [(weights[at] * share).astype(BF) if at in weights else nothing for at in places], axis=1
            )
        )
    result = jnp.dot(jnp.concatenate(rows, axis=0), v, preferred_element_type=F32).astype(BF)
    for r in range(2):
        o_ref[j, f, r, query_rows, :] = result[r * HALF : (r + 1) * HALF]


def step_kernel(
    factor, radius_ref, q_hbm, k_hbm, v_hbm, w_hbm, g_hbm, down_hbm, up_hbm,
    mixed_hbm, back_hbm, grads_hbm,
    mixed_ref, back_ref,
    qs_ref, ks_ref, vs_ref, os_ref, w_ref, g_ref, att_ref,
    part_ref, ra_ref, acc_ref, rb_ref, rd_ref, rounded_ref, fin_ref,
    down_ref, up_ref, own_back_ref, back_low_ref, back_turned_ref, down_part_ref, down_got_ref,
    load_sem, out_sem, in_sem, halo_out, halo_in, o_in, p_sem,
    w_out, wx_in, wy_in, wz_in, ws_in, r_sem, e_in, store_sem,
):
    z, xh, y, xl, core = place()
    x = xh * 2 + xl
    here = xl == core
    ring = x * 2 + core
    band = y * 2 + core
    before, after = (band + 7) % 8, (band + 1) % 8
    left = device(z, x, before // 2, before % 2)
    right = device(z, x, after // 2, after % 2)
    sibling = device(z, x, y, 1 - core)

    def ring_device(step):
        other = (ring + step) % 8
        return other // 2, other % 2, device(z, other // 2, y, other % 2)

    def y_device(step):
        return device(z, x, (y + step) % 4, core)

    def z_device(step):
        return device((z + step) % 4, x, y, core)

    up, down = z_device(3), z_device(1)

    def head_columns(chip, j):
        return pl.ds(pl.multiple_of((chip * GROUP_HEADS + j) * HEAD_DIM, HEAD_DIM), HEAD_DIM)

    load_gradient = pltpu.make_async_copy(g_hbm, g_ref, load_sem.at[0])
    load_weight = [
        pltpu.make_async_copy(
            w_hbm.at[:, group_columns((z + quarter) % 4)],
            w_ref.at[y * 2 + xl, core, :, group_columns((z + quarter) % 4)],
            load_sem.at[1 + quarter // 2],
        )
        for quarter in (0, 2)
    ]
    load_up = pltpu.make_async_copy(up_hbm, up_ref, load_sem.at[3])
    load_down = pltpu.make_async_copy(down_hbm, down_ref, load_sem.at[4])
    load_gradient.start()
    load_up.start()
    load_down.start()
    for copy in load_weight:
        copy.start()

    outside = (band + 7 + 2 * core) % 8
    enter(
        [ring_device(step)[2] for step in range(1, 8)]
        + [device((z + step % 4) % 4, x, (y + step // 4) % 4, core) for step in range(1, 16)]
        + [device(z, x, outside // 2, outside % 2)]
    )

    arrays = ((k_hbm, ks_ref, 1), (v_hbm, vs_ref, 1), (q_hbm, qs_ref, 0))

    def exchange(i, j, step):
        src, dst, pad = arrays[i]
        target = (x + step) % CHIPS
        piece = src.at[:, 0, :, head_columns(target, j)]
        slot = dst.at[j, pl.ds(pad + 2 * xh, 2), pad + core]
        return piece, slot, remote(
            piece, slot, out_sem.at[0], in_sem.at[i, j],
            device(z, target, y, xl),
        )

    def give(i, j):
        for step in (2, 1, 3):
            exchange(i, j, step)[2].start()
        piece, slot, copy = exchange(i, j, 0)

        @pl.when(here)
        def _():
            pltpu.make_async_copy(piece, slot, in_sem.at[i, j]).start()

        @pl.when(jnp.logical_not(here))
        def _():
            copy.start()

    def landed(i, j):
        own = (pl.ds(1, 4), pl.ds(1, 2)) if i < 2 else ()
        arrived(arrays[i][1].at[(j, *own)], in_sem.at[i, j])

    def halos(i, j):
        ref = arrays[i][1].at[j]

        def send(n, src, dst, target):
            return remote(src, dst, halo_out.at[i], halo_in.at[i, j, min(n // 2, 1)], target)

        rows, own = pl.ds(1, 2), pl.ds(1, 4)
        return (
            send(0, ref.at[1, rows], ref.at[5, rows], up),
            send(1, ref.at[4, rows], ref.at[0, rows], down),
            send(2, ref.at[own, 1], ref.at[own, 3], left),
            send(3, ref.at[own, 2], ref.at[own, 0], right),
            send(4, ref.at[0, 1], ref.at[0, 3], left),
            send(5, ref.at[5, 1], ref.at[5, 3], left),
            send(6, ref.at[0, 2], ref.at[0, 0], right),
            send(7, ref.at[5, 2], ref.at[5, 0], right),
        )

    def start_halos(j):
        for i in range(2):
            landed(i, j)
            for copy in halos(i, j)[:4]:
                copy.start()

    def start_corners(j):
        for i in range(2):
            arrived(arrays[i][1].at[j, 0], halo_in.at[i, j, 0])
            for copy in halos(i, j)[4:]:
                copy.start()

    def await_head(j):
        for i in range(2):
            arrived(arrays[i][1].at[j, pl.ds(0, 3)], halo_in.at[i, j, 1])
        landed(2, j)

    def attend_frames(j, first, last, midway=None):
        head = x * GROUP_HEADS + j
        radii = [radius_ref[n, head] for n in range(3)]

        def one(f, carry):
            if midway is not None:
                pl.when(f == 2)(midway)
            for half in range(2):
                attend(
                    j, f, half, radii, z * 4 + f, y * 4 + core * 2, qs_ref, ks_ref, vs_ref, os_ref
                )
            return carry

        lax.fori_loop(first, last, one, 0)

    def give_back(j, n):
        frames = (xh + n // 2) % 2
        row = (core + n % 2) % 2
        piece = os_ref.at[j, pl.ds(2 * frames, 2), row]
        slot = att_ref.at[:, :, head_columns(x, j)]
        return piece, slot, remote(
            piece, slot, out_sem.at[1], o_in.at[0], device(z, frames * 2 + core, y, row)
        )

    def start_back(j, near=True, far=True):
        if far:
            give_back(j, 2)[2].start()
            give_back(j, 3)[2].start()
        if not near:
            return
        give_back(j, 1)[2].start()
        piece, slot, copy = give_back(j, 0)

        @pl.when(here)
        def _():
            pltpu.make_async_copy(piece, slot, o_in.at[0]).start()

        @pl.when(jnp.logical_not(here))
        def _():
            copy.start()

    def weight_piece(quarter, n, side):
        return w_ref.at[pl.ds(2 * ((y + n) % 4), 2), side, :, group_columns((z + quarter) % 4)]

    def weight_shard(quarter, n, part):
        return w_ref.at[
            2 * ((y + n) % 4) + (xl + part) % 2, core, :, group_columns((z + quarter) % 4)
        ]

    weight_x = remote(
        weight_shard(0, 0, 0), weight_shard(0, 0, 0), w_out.at[0], wx_in.at[0],
        device(z, (xh + core) % 2 * 2 + 1 - xl, y, core),
    )
    weight_across = remote(
        weight_shard(0, 0, 1), weight_shard(0, 0, 1), w_out.at[0], wx_in.at[1], z_device(2)
    )

    def weight_y(quarter, step, part):
        piece = weight_shard(quarter, 0, part)
        at = quarter // 2
        return remote(
            piece, piece, w_out.at[1], wy_in.at[at, 3 - step],
            y_device(step),
        )

    def weight_z(way, n, part):
        piece = weight_shard(0, n, part)
        return remote(piece, piece, w_out.at[2], wz_in.at[way, n], (up, down)[way])

    def weight_sibling(quarter, n):
        piece = weight_piece(quarter, n, core)
        return remote(piece, piece, w_out.at[3], ws_in.at[0], sibling)

    def start_y(quarter, part, steps=(1, 3, 2)):
        for step in steps:
            weight_y(quarter, step, part).start()

    def start_z(n, part):
        for way in range(2):
            weight_z(way, n, part).start()

    def take_y(quarter, n):
        arrived(weight_piece(quarter, n, core), wy_in.at[quarter // 2, n - 1])
        weight_sibling(quarter, n).start()

    def take_z(n):
        for way, quarter in ((0, 1), (1, 3)):
            arrived(weight_piece(quarter, n, core), wz_in.at[way, n])
            weight_sibling(quarter, n).start()

    def give_low(step):
        target = (x + step) % CHIPS
        return remote(
            own_back_ref, back_low_ref.at[xh, core], out_sem.at[2], o_in.at[1],
            device(z, target, y, xl),
        )

    def add_down(j):
        total = jnp.zeros((RANK, HEAD_DIM), F32)
        for f in range(4):
            for r in range(2):
                total = total + jnp.dot(
                    back_turned_ref[f, r], os_ref[j, f, r], preferred_element_type=F32
                )
        down_part_ref[:, j * HEAD_DIM : (j + 1) * HEAD_DIM] = factor * total

    def half_rows(n):
        return pl.ds(pl.multiple_of(n * 32, 32), 32)

    down_to_sibling = remote(
        down_part_ref.at[half_rows(1 - core)], down_got_ref, p_sem.at[0], p_sem.at[1], sibling
    )

    def start_sum(a):
        for step in range(1, 16):
            sum_copy(a, step).start()
        rb_ref[a, y * 4 + z] = acc_ref[a, y]

    def sum_copy(a, step):
        dy, dz = step // 4, step % 4
        return remote(
            acc_ref.at[a, (y + dy) % 4], rb_ref.at[a, y * 4 + z], r_sem.at[a, 0], r_sem.at[a, 1],
            device((z + dz) % 4, x, (y + dy) % 4, core),
        )

    def round_y(a, step):
        return remote(
            rd_ref.at[a, y], rd_ref.at[a, y], r_sem.at[a, 2], r_sem.at[a, 3], y_device(step)
        )

    def finish_sum(a):
        arrived(rb_ref.at[a, pl.ds(0, 15)], r_sem.at[a, 1])
        total = rb_ref[a, 0]
        for source in range(1, 16):
            total = total + rb_ref[a, source]
        rd_ref[a, y] = total
        for step in range(1, 4):
            round_y(a, step).start()

    def share(a, tx, tc):
        return fin_ref.at[a, half_rows(tc), group_columns(tx)]

    def round_x(a, step):
        return remote(
            rounded_ref.at[a], share(a, x, core), r_sem.at[a, 4], e_in.at[a, step],
            device(z, (x + step) % CHIPS, y, core),
        )

    def pass_share(a, step):
        piece = share(a, (x + CHIPS - step) % CHIPS, core)
        return remote(piece, piece, r_sem.at[a, 5], e_in.at[a, 0], sibling)

    def start_round(a):
        arrived(rb_ref.at[a, pl.ds(0, 3)], r_sem.at[a, 3])
        rounded_ref[a] = rd_ref[a].reshape(32, GROUP).astype(BF)
        for step in (2, 1, 3):
            round_x(a, step).start()
        fin_ref[a, half_rows(core), group_columns(x)] = rounded_ref[a]
        pass_share(a, 0).start()

    def pass_round(a):
        for step in (1, 3, 2):
            arrived(share(a, (x + CHIPS - step) % CHIPS, core), e_in.at[a, step])
            pass_share(a, step).start()

    def finish_round(a):
        arrived(fin_ref.at[a, half_rows(1 - core)], e_in.at[a, 0])
        arrived(rb_ref.at[a, pl.ds(0, 15)], r_sem.at[a, 0])
        arrived(rb_ref.at[a, pl.ds(0, 3)], r_sem.at[a, 2])
        arrived(fin_ref.at[a, pl.ds(0, 32), pl.ds(0, 3 * GROUP)], r_sem.at[a, 4])
        arrived(fin_ref.at[a, pl.ds(0, 32)], r_sem.at[a, 5])

    K, V, Q = 0, 1, 2
    for copy in load_weight:
        copy.wait()
    weight_x.start()
    start_y(0, 0)
    start_z(0, 0)
    give(K, 0)
    give(V, 0)
    load_gradient.wait()
    load_up.wait()
    load_down.wait()
    contract_last = (((1,), (1,)), ((), ()))
    contract_first = (((0,), (0,)), ((), ()))
    tokens = 2 * COLS
    low_back = lax.dot_general(
        g_ref[...].reshape(tokens, WIDTH), up_ref[...], contract_last, preferred_element_type=F32
    ).astype(BF)
    own_back_ref[...] = jnp.concatenate([low_back[:COLS], low_back[COLS:]], axis=1)
    for step in (2, 1, 3):
        give_low(step).start()
    low_copy = give_low(0)
    low_slot = back_low_ref.at[xh, core]

    @pl.when(here)
    def _():
        pltpu.make_async_copy(own_back_ref, low_slot, o_in.at[1]).start()

    @pl.when(jnp.logical_not(here))
    def _():
        low_copy.start()

    for i, j in (
        (K, 1), (V, 1), (Q, 0), (K, 2), (V, 2), (Q, 1),
        (K, 3), (V, 3), (Q, 2), (K, 4), (V, 4), (Q, 3), (Q, 4),
    ):
        give(i, j)
    weight_x.wait_recv()
    start_y(0, 1)
    start_z(0, 1)
    weight_sibling(0, 0).start()

    start_halos(0)
    start_corners(0)
    take_y(0, 1)
    start_z(1, 0)
    start_halos(1)
    arrived(back_low_ref, o_in.at[1])
    for pair in range(2):
        for row in range(2):
            turned = back_low_ref[pair, row].astype(F32).T.astype(BF)
            for n in range(2):
                frame = 2 * pair + n
                back_turned_ref[frame, row] = turned[n * RANK : (n + 1) * RANK]
    await_head(0)
    start_z(1, 1)
    start_y(2, 0, (1, 3))
    attend_frames(0, 0, 4, functools.partial(start_corners, 1))
    start_back(0)
    add_down(0)

    start_halos(2)
    await_head(1)
    start_y(2, 0, (2,))
    weight_across.start()
    take_z(0)
    attend_frames(1, 0, 4, functools.partial(start_corners, 2))
    start_back(1)
    add_down(1)

    start_halos(3)
    await_head(2)
    arrived(weight_shard(2, 0, 1), wx_in.at[1])
    weight_sibling(2, 0).start()
    start_y(2, 1, (1, 3))
    take_y(0, 3)
    start_z(3, 0)
    take_z(1)
    attend_frames(2, 0, 4, functools.partial(start_corners, 3))
    start_back(2)
    add_down(2)

    start_halos(4)
    await_head(3)
    start_y(2, 1, (2,))
    start_z(3, 1)
    take_y(0, 2)
    start_z(2, 0)
    start_z(2, 1)
    attend_frames(3, 0, 4, functools.partial(start_corners, 4))
    start_back(3)
    add_down(3)
    for n in range(1, 4):
        take_y(2, n)
    await_head(4)
    far_frames = 2 * (1 - xh)
    attend_frames(4, far_frames, far_frames + 2)
    start_back(4, near=False)
    attend_frames(4, 2 - far_frames, 4 - far_frames)
    start_back(4, far=False)
    add_down(4)
    down_to_sibling.start()
    take_z(3)
    take_z(2)

    step_width = 256

    def forward(j, carry):
        columns = pl.ds(pl.multiple_of(j * step_width, step_width), step_width)
        frozen = jnp.dot(
            att_ref[...].reshape(tokens, WIDTH), w_ref[:, :, :, columns].reshape(WIDTH, step_width),
            preferred_element_type=F32,
        )
        adapter = jnp.dot(low, up_ref[:, columns], preferred_element_type=F32)
        mixed_ref[:, :, columns] = (
            (frozen + ADAPTER_SCALE * adapter).astype(BF).reshape(2, COLS, step_width)
        )
        return carry

    def backward(j, carry):
        rows = group_columns(j)
        frozen = lax.dot_general(
            g_ref[...].reshape(tokens, WIDTH), w_ref[pl.ds(2 * j, 2)].reshape(GROUP, WIDTH),
            contract_last, preferred_element_type=F32,
        )
        adapter = jnp.dot(low_back, down_ref[:, rows], preferred_element_type=F32)
        back_ref[:, :, rows] = (
            (frozen + ADAPTER_SCALE * adapter).astype(BF).reshape(2, COLS, GROUP)
        )
        return carry

    down_to_sibling.wait_recv()
    acc_ref[1] = (down_part_ref[half_rows(core), :] + down_got_ref[...]).reshape(4, 8, GROUP)
    start_sum(1)

    arrived(att_ref, o_in.at[0])
    low = lax.dot_general(
        att_ref[...].reshape(tokens, WIDTH), down_ref[...], contract_last, preferred_element_type=F32
    ).astype(BF)
    low_turned = low.astype(F32).T.astype(BF)

    def phase_a(dx, dc):
        tx, tc = (x + dx) % CHIPS, (core + dc) % 2
        return remote(
            part_ref.at[half_rows(tc), group_columns(tx)], ra_ref.at[2 * dx + dc - 1],
            p_sem.at[2], p_sem.at[3], device(z, tx, y, tc),
        )

    for dx in (2, 1, 3, 0):
        columns = group_columns((x + dx) % CHIPS)
        part_ref[:, columns] = (
            factor
            * jnp.dot(
                low_turned, g_ref[:, :, columns].reshape(tokens, GROUP), preferred_element_type=F32
            )
        ).astype(BF)
        for dc in range(2):
            if dx + dc > 0:
                phase_a(dx, dc).start()

    blocks = WIDTH // step_width
    arrived(w_ref.at[:, 1 - core], ws_in.at[0])
    lax.fori_loop(0, blocks // 2, forward, 0)
    @pl.when(here)
    def _():
        arrived(ks_ref.at[:, :, pl.ds(0, 3)], out_sem.at[0])
        arrived(qs_ref.at[:, pl.ds(0, 3)], out_sem.at[1])
        arrived(ks_ref.at[0, 0, pl.ds(0, 3)], out_sem.at[2])

    @pl.when(jnp.logical_not(here))
    def _():
        arrived(ks_ref, out_sem.at[0])
        arrived(qs_ref, out_sem.at[1])
        arrived(back_low_ref, out_sem.at[2])

    for i in range(2):
        arrived(arrays[i][1].at[:, pl.ds(0, 4)], halo_out.at[i])
    arrived(w_ref.at[0, :, :, pl.ds(0, GROUP)], w_out.at[0])
    arrived(w_ref.at[pl.ds(0, 6), :, :, pl.ds(0, GROUP)], w_out.at[1])
    arrived(w_ref.at[:, :, :, pl.ds(0, GROUP)], w_out.at[2])
    arrived(w_ref.at[:, :, :, pl.ds(0, 2 * GROUP)], w_out.at[3])
    down_to_sibling.wait_send()
    total = part_ref[half_rows(core), group_columns(x)].astype(F32)
    arrived(ra_ref, p_sem.at[3])
    for step in range(1, 8):
        total = total + ra_ref[step - 1].astype(F32)
    acc_ref[0] = total.reshape(4, 8, GROUP)
    start_sum(0)
    finish_sum(1)
    lax.fori_loop(blocks // 2, blocks, forward, 0)
    store_mixed = pltpu.make_async_copy(mixed_ref, mixed_hbm, store_sem.at[1])
    store_mixed.start()
    lax.fori_loop(0, 2, backward, 0)
    finish_sum(0)
    start_round(1)
    lax.fori_loop(2, 3, backward, 0)
    start_round(0)
    pass_round(1)
    lax.fori_loop(3, CHIPS, backward, 0)
    store_back = pltpu.make_async_copy(back_ref, back_hbm, store_sem.at[0])
    store_back.start()
    store_grads = [
        pltpu.make_async_copy(fin_ref.at[a], grads_hbm.at[a], store_sem.at[2 + a]) for a in range(2)
    ]
    pass_round(0)
    finish_round(1)
    store_grads[1].start()
    finish_round(0)
    store_grads[0].start()
    arrived(ra_ref, p_sem.at[2])
    store_back.wait()
    store_mixed.wait()
    store_grads[1].wait()
    store_grads[0].wait()


def deliver_kernel(
    mixed_hbm, back_hbm, grads_hbm, mixed_out, back_out, grad_up_out, grad_down_out,
    held_ref, grads_ref, wide_ref, take_sem, put_sem,
):
    takes = [pltpu.make_async_copy(grads_hbm, grads_ref, take_sem.at[0])]
    puts = []
    for f in range(2):
        for n, (src, dst) in enumerate(((mixed_hbm, mixed_out), (back_hbm, back_out))):
            for half in range(2):
                at = 2 + 4 * f + 2 * n + half
                rows = pl.ds(half * HALF, HALF)
                held = held_ref.at[n, f, rows]
                takes.append(pltpu.make_async_copy(src.at[f, rows], held, take_sem.at[at]))
                puts.append(pltpu.make_async_copy(held, dst.at[f, rows], put_sem.at[at]))
    for copy in takes:
        copy.start()
    for n, dst in enumerate((grad_up_out, grad_down_out)):
        if n == 0:
            takes[0].wait()
        wide_ref[n] = grads_ref[n].astype(F32)
        copy = pltpu.make_async_copy(wide_ref.at[n], dst, put_sem.at[n])
        copy.start()
        puts.append(copy)
    for take, put in zip(takes[1:], puts[:8]):
        take.wait()
        put.start()
    for copy in puts:
        copy.wait()


def per_device(
    queries, keys, values, head_window_radius, output_weight, adapter_down_weight, adapter_up_weight,
    output_gradient,
):
    factor = ADAPTER_SCALE / math.sqrt(GRID * GRID * COLS)
    smem = pl.BlockSpec(memory_space=pltpu.SMEM)
    hbm = pl.BlockSpec(memory_space=pl.ANY)
    block = jax.ShapeDtypeStruct((2, COLS, WIDTH), BF)
    dma = pltpu.SemaphoreType.DMA
    small = jax.ShapeDtypeStruct((RANK, WIDTH), F32)
    mixed, back, grads = pl.pallas_call(
        functools.partial(step_kernel, factor),
        out_shape=(block, block, jax.ShapeDtypeStruct((2, RANK, WIDTH), BF)),
        in_specs=[smem, hbm, hbm, hbm, hbm, hbm, hbm, hbm],
        out_specs=(hbm,) * 3,
        scratch_shapes=[
            pltpu.VMEM((2, COLS, WIDTH), BF),
            pltpu.VMEM((2, COLS, WIDTH), BF),
            pltpu.VMEM((GROUP_HEADS, 4, 2, COLS, HEAD_DIM), BF),
            pltpu.VMEM((GROUP_HEADS, 6, 4, COLS, HEAD_DIM), BF),
            pltpu.VMEM((GROUP_HEADS, 6, 4, COLS, HEAD_DIM), BF),
            pltpu.VMEM((GROUP_HEADS, 4, 2, COLS, HEAD_DIM), BF),
            pltpu.VMEM((8, 2, COLS, WIDTH), BF),
            pltpu.VMEM((2, COLS, WIDTH), BF),
            pltpu.VMEM((2, COLS, WIDTH), BF),
            pltpu.VMEM((RANK, WIDTH), BF),
            pltpu.VMEM((7, 32, GROUP), BF),
            pltpu.VMEM((2, 4, 8, GROUP), F32),
            pltpu.VMEM((2, 16, 8, GROUP), F32),
            pltpu.VMEM((2, 4, 8, GROUP), F32),
            pltpu.VMEM((2, 32, GROUP), BF),
            pltpu.VMEM((2, RANK, WIDTH), BF),
            pltpu.VMEM((RANK, WIDTH), BF),
            pltpu.VMEM((RANK, WIDTH), BF),
            pltpu.VMEM((COLS, 2 * RANK), BF),
            pltpu.VMEM((2, 2, COLS, 2 * RANK), BF),
            pltpu.VMEM((4, 2, RANK, COLS), BF),
            pltpu.VMEM((RANK, GROUP), F32),
            pltpu.VMEM((32, GROUP), F32),
            dma((5,)), dma((3,)), dma((3, GROUP_HEADS)), dma((2,)), dma((2, GROUP_HEADS, 2)),
            dma((2,)), dma((4,)),
            dma((4,)), dma((2,)), dma((2, 3)), dma((2, 4)), dma((1,)), dma((2, 6)), dma((2, 4)), dma((4,)),
        ],
        compiler_params=pltpu.CompilerParams(
            collective_id=0, has_side_effects=True, vmem_limit_bytes=57 * 2**20
        ),
        cost_estimate=pl.CostEstimate(
            flops=14_000_000_000, bytes_accessed=100_000_000, transcendentals=7_000_000
        ),
        name="training_step",
    )(
        head_window_radius.T, queries, keys, values, output_weight,
        output_gradient.reshape(2, COLS, WIDTH), adapter_down_weight.T, adapter_up_weight,
    )
    mixed, back, grad_up, grad_down = pl.pallas_call(
        deliver_kernel,
        out_shape=(block, block, small, small),
        in_specs=[hbm] * 3,
        out_specs=(hbm,) * 4,
        scratch_shapes=[
            pltpu.VMEM((2, 2, COLS, WIDTH), BF),
            pltpu.VMEM((2, RANK, WIDTH), BF),
            pltpu.VMEM((2, RANK, WIDTH), F32),
            dma((10,)),
            dma((10,)),
        ],
        compiler_params=pltpu.CompilerParams(vmem_limit_bytes=60 * 2**20),
        name="deliver",
    )(mixed, back, grads)
    shape = (2, 1, COLS, WIDTH)
    return mixed.reshape(shape), back.reshape(shape), grad_up, grad_down.T


def solution(mesh):
    tokens = P("tm", "height", None, None)
    return jax.shard_map(
        per_device,
        mesh=mesh,
        in_specs=(tokens, tokens, tokens, P(), P("height", None), P(), P(), tokens),
        out_specs=(tokens, tokens, P(), P()),
        check_vma=False,
    )
```
